32 devices in a mesh: dp: 8 (over y, x, core), ctx: 4 (over z).
Axes of the slice: x: 2, y: 2, z: 4, core: 2. Of those that a mesh axis runs over, the one named last changes fastest.
Arguments:
- layer_input: bfloat16 [16384, 1152], P(('dp', 'ctx')), may hold values from -6 to 6
- cotangent: bfloat16 [16384, 1152], P(('dp', 'ctx')), may hold values from -6 to 6
- lengths: int32 [8], P('dp'), may hold values from 1537 to 2048, as said below
- weights: float32 [1152, 23296], P(('dp', 'ctx'))
- norm_gains: float32 [1152, 4], P(('dp', 'ctx')), may hold values from -0.4 to 0.4
- head_gains: float32 [256, 2], P(('dp', 'ctx')), may hold values from -0.2 to 0.2
- moment_weights: float32 [1152, 23296], P(('dp', 'ctx')), may hold values from -38.4 to 38.4
- moment_gains: float32 [1152, 4], P(('dp', 'ctx')), may hold values from -38.4 to 38.4
- moment_head: float32 [256, 2], P(('dp', 'ctx')), may hold values from -38.4 to 38.4
- square_weights: float32 [1152, 23296], P(('dp', 'ctx')), may hold values from 425.984 to 1638.4
- square_gains: float32 [1152, 4], P(('dp', 'ctx')), may hold values from 425.984 to 1638.4
- square_head: float32 [256, 2], P(('dp', 'ctx')), may hold values from 13107.2 to 52428.8
Outputs:
- output: bfloat16 [16384, 1152], P(('dp', 'ctx'))
- grad_input: bfloat16 [16384, 1152], P(('dp', 'ctx'))
- new_weights: float32 [1152, 23296], P(('dp', 'ctx'))
- new_gains: float32 [1152, 4], P(('dp', 'ctx'))
- new_head_gains: float32 [256, 2], P(('dp', 'ctx'))
- first_weights: float32 [1152, 23296], P(('dp', 'ctx'))
- first_gains: float32 [1152, 4], P(('dp', 'ctx'))
- first_head: float32 [256, 2], P(('dp', 'ctx'))
- second_weights: float32 [1152, 23296], P(('dp', 'ctx'))
- second_gains: float32 [1152, 4], P(('dp', 'ctx'))
- second_head: float32 [256, 2], P(('dp', 'ctx'))
- weights_bf16: bfloat16 [1152, 23296], P(('dp', 'ctx'))
The draws below stay inside these ranges and needn't reach their ends.
Inputs may be any that keep to these rules, and one draw needn't show every extreme that they name: `lengths`: each sequence has at least 1537 valid tokens; in every draw some sequence is full.
All inputs are finite; a program needn't handle non-finite values.
Results may differ from the reference program's by a relative error of at most 0.019.
Values may be sent and summed in bfloat16 or wider, within the bound.
No kernel may reach another device: no remote copies, remote signals or barrier semaphores. Data moves between devices by JAX's collectives and lax.ppermute only.
A program may use at most 448 MiB of HBM per device.

```python
import math
import jax
import jax.numpy as jnp
from jax import lax

D = 1152
H = 4
HD = 256
FF = 6912
TOK_DEV = 512
STEP = 10
SEQ = 2048
TOKENS = 16384
WCOLS = 23296
N_DP = 8
N_CTX = 4


def draw_lengths(key, part):
    key = jax.random.fold_in(key, 5)
    first_key, second_key = jax.random.split(key)
    seq_slots = TOK_DEV * N_CTX
    shorter = seq_slots - jax.random.randint(first_key, (N_DP,), 0, TOK_DEV)
    chosen = jax.random.randint(second_key, (), 0, N_DP)
    return jnp.where(jnp.arange(N_DP) == chosen, seq_slots, shorter).astype(jnp.int32)


def draw_weights(key, part):
    key = jax.random.fold_in(key, 11)
    q_cols = H * HD
    columns = jnp.arange(2 * q_cols + 2 * HD + 3 * FF)
    start_out = q_cols + 2 * HD + 2 * FF
    start_down = start_out + q_cols
    scale = jnp.where(columns < start_out, D ** (-0.5), jnp.where(columns < start_down, q_cols ** (-0.5), FF ** (-0.5))).astype(jnp.float32)
    return jax.random.normal(key, (D, columns.shape[0]), jnp.float32) * scale[None, :]


def block_levels(own_key, dims, cuts, smallest, top_value):
    factor_of, own = 1.0, jax.random.fold_in(own_key, 6)
    for axis_at, blocks in cuts:
        draws = jnp.exp(jax.random.uniform(jax.random.fold_in(own, axis_at), (blocks,), jnp.float32, smallest / len(cuts), top_value / len(cuts)))
        factor_of = factor_of * jnp.repeat(draws, dims[axis_at] // blocks).reshape([-1 if axis == axis_at else 1 for axis in range(len(dims))])
    return factor_of


def centred(key, shape, spread, reach, shards=(), held_as=jnp.bfloat16):
    values = spread * jax.random.normal(key, shape, jnp.float32)
    if shards:
        values = values * block_levels(key, shape, shards, -0.22, 0.18)
    return jnp.clip(values, -reach, reach).astype(held_as)


def setup_inputs(seed: int = 0) -> dict:
    key_list = jax.random.split(jax.random.key(seed), 13)
    layer_input = centred(key_list[0], (TOKENS, D), 1.0, 6.0, ((0, 32),))
    cotangent = centred(key_list[1], (TOKENS, D), 1.0, 6.0, ((0, 32),))
    lengths = draw_lengths(jax.random.fold_in(key_list[12], 71), 0)
    weights = draw_weights(jax.random.fold_in(key_list[12], 71), 0)
    norm_gains = centred(key_list[4], (D, 4), 0.1, 0.4, ((0, 32),), jnp.float32)
    head_gains = centred(key_list[5], (HD, 2), 0.05, 0.2, ((0, 32),), jnp.float32)
    moment_weights = centred(key_list[6], (D, WCOLS), (0.078 * TOKENS ** 0.5), 38.4, ((0, 32),), jnp.float32)
    moment_gains = centred(key_list[7], (D, 4), (0.078 * TOKENS ** 0.5), 38.4, ((0, 32),), jnp.float32)
    moment_head = centred(key_list[8], (HD, 2), (0.078 * TOKENS ** 0.5), 38.4, ((0, 32),), jnp.float32)
    square_weights = jnp.clip(jnp.exp(math.log(1638.4) - 1.34707364 * jax.random.uniform(key_list[9], (D, WCOLS), jnp.float32) ** block_levels(key_list[9], (D, WCOLS), ((0, 32),), -0.2, 0.2)), 425.984, 1638.4)
    square_gains = jnp.clip(jnp.exp(math.log(1638.4) - 1.34707364 * jax.random.uniform(key_list[10], (D, 4), jnp.float32) ** block_levels(key_list[10], (D, 4), ((0, 32),), -0.2, 0.2)), 425.984, 1638.4)
    square_head = jnp.clip(jnp.exp(math.log(52428.8) - 1.3862944 * jax.random.uniform(key_list[11], (HD, 2), jnp.float32) ** block_levels(key_list[11], (HD, 2), ((0, 32),), -0.2, 0.2)), 13107.2, 52428.8)
    return {"layer_input": layer_input, "cotangent": cotangent, "lengths": lengths, "weights": weights, "norm_gains": norm_gains, "head_gains": head_gains, "moment_weights": moment_weights, "moment_gains": moment_gains, "moment_head": moment_head, "square_weights": square_weights, "square_gains": square_gains, "square_head": square_head}


@jax.custom_vjp
def low(v):
    return lax.optimization_barrier(v.astype(jnp.bfloat16)).astype(jnp.float32)

@jax.custom_vjp
def low_back(v):
    return v

def low_keep(v):
    return (low(v), None)

def low_pass(kept, grad):
    return (grad,)

def back_keep(v):
    return (v, None)

def back_low(kept, grad):
    return (low(grad),)
low.defvjp(low_keep, low_pass)
low_back.defvjp(back_keep, back_low)
NORM_EPS = 1e-06
ROPE_BASE = 1000000.0
QUERY_SCALE = 0.0625
BETA_ONE = 0.9
BETA_TWO = 0.95
ADAM_EPS = 1e-08
RATE_WEIGHTS = 0.03
RATE_GAINS = 0.1
WEIGHT_DECAY = 0.1
NEG_LARGE = -1e+30

def block_positions(slots, rows, count):
    half_rows = rows // 2
    device = slots // rows
    within = slots % rows
    block = jnp.where(within < half_rows, device, 2 * count - 1 - device)
    return (block * half_rows + within % half_rows).astype(jnp.int32)

def rms_gain(values, gain):
    return values * lax.rsqrt(lax.optimization_barrier(jnp.mean(values * values, axis=-1, keepdims=True)) + NORM_EPS) * gain

def rotate(values, positions):
    half_dim = values.shape[-1] // 2
    freqs = jnp.power(ROPE_BASE, -2.0 * jnp.arange(half_dim).astype(jnp.float32) / values.shape[-1])
    angles = positions.astype(jnp.float32)[:, None] * freqs[None, :]
    cosine = jnp.cos(angles)[:, None, :]
    sine = jnp.sin(angles)[:, None, :]
    first = values[..., :half_dim]
    second = values[..., half_dim:]
    return jnp.concatenate([first * cosine - second * sine, second * cosine + first * sine], axis=-1)

def geglu(gate_up):
    return jax.nn.gelu(gate_up[:, :FF], approximate=True) * gate_up[:, FF:]

def offsets():
    q_cols = H * HD
    start_gate = q_cols + 2 * HD
    start_out = start_gate + 2 * FF
    start_down = start_out + q_cols
    return (q_cols, start_gate, start_out, start_down)

def matmul_high(left, right):
    return jnp.dot(left, right, precision=lax.Precision.HIGHEST, preferred_element_type=jnp.float32)

def attend(queries, keys, values, positions, key_valid):
    block_rows = min(512, SEQ)
    blocks = SEQ // block_rows

    def one_block(block_in):
        query_block, query_pos = block_in
        scores = jnp.einsum('thd,sd->hts', query_block, keys, precision=lax.Precision.HIGHEST)
        scores = low_back(scores)
        allowed = (positions[None, :] <= query_pos[:, None]) & key_valid[None, :]
        scores = jnp.where(allowed[None], scores, NEG_LARGE)
        row_max = lax.optimization_barrier(jnp.max(scores, axis=-1, keepdims=True))
        expon = jnp.exp(scores - row_max)
        weights_row = low(expon / lax.optimization_barrier(jnp.sum(expon, axis=-1, keepdims=True)))
        mixed = jnp.einsum('hts,sd->thd', weights_row, values, precision=lax.Precision.HIGHEST)
        return mixed.reshape(block_rows, H * HD)
    result = lax.map(jax.checkpoint(one_block), (queries.reshape(blocks, block_rows, H, HD), positions.reshape(blocks, block_rows)))
    return result.reshape(SEQ, H * HD)

def layer(inputs, weights, norm_params, head_params, positions, key_valid):
    q_cols, start_gate, start_out, start_down = offsets()
    norm_gains = 1.0 + norm_params
    head_gains = 1.0 + head_params
    normed_in = low(rms_gain(inputs, norm_gains[:, 0]))
    projected = low_back(matmul_high(normed_in, weights[:, :start_gate]))
    query_raw = projected[:, :q_cols].reshape(SEQ, H, HD)
    key_raw = projected[:, q_cols:q_cols + HD]
    value_raw = projected[:, q_cols + HD:start_gate]
    queries = low(rotate(rms_gain(query_raw, head_gains[:, 0]), positions) * QUERY_SCALE)
    keys = low(rotate(rms_gain(key_raw[:, None, :], head_gains[:, 1]), positions)[:, 0])
    values = low(value_raw)
    mixed = low(low_back(attend(queries, keys, values, positions, key_valid)))
    attn_proj = low_back(matmul_high(mixed, weights[:, start_out:start_down].T))
    residual_mid = inputs + rms_gain(attn_proj, norm_gains[:, 1])
    normed_mid = low(rms_gain(residual_mid, norm_gains[:, 2]))
    gate_up = low_back(matmul_high(normed_mid, weights[:, start_gate:start_out]))
    hidden = low(geglu(gate_up))
    mlp_proj = low_back(matmul_high(hidden, weights[:, start_down:].T))
    return residual_mid + rms_gain(mlp_proj, norm_gains[:, 3])

def adamw(weight, grad, first, second, rate, decay):
    first_new = BETA_ONE * first + (1.0 - BETA_ONE) * grad
    second_new = BETA_TWO * second + (1.0 - BETA_TWO) * grad * grad
    update = first_new / (1.0 - BETA_ONE ** STEP) / (jnp.sqrt(second_new / (1.0 - BETA_TWO ** STEP)) + ADAM_EPS)
    return (weight - rate * (update + decay * weight), first_new, second_new)

def reference(layer_input, cotangent, lengths, weights, norm_gains, head_gains, moment_weights, moment_gains, moment_head, square_weights, square_gains, square_head):
    weights_low = low(weights)
    gains_low = low(norm_gains)
    head_low = low(head_gains)
    positions = block_positions(jnp.arange(SEQ, dtype=jnp.int32), TOK_DEV, N_CTX)

    def per_sequence(totals, seq_in):
        seq_input, seq_cot, seq_length = seq_in
        key_valid = positions < seq_length

        def forward(inputs, weight_arg, gain_arg, head_arg):
            return layer(inputs, weight_arg, gain_arg, head_arg, positions, key_valid)
        result, pullback = jax.vjp(forward, seq_input.astype(jnp.float32), weights_low, gains_low, head_low)
        out_grad = seq_cot.astype(jnp.float32) * key_valid[:, None].astype(jnp.float32)
        grad_x, grad_w, grad_g, grad_h = pullback(out_grad)
        totals = (totals[0] + grad_w, totals[1] + grad_g, totals[2] + grad_h)
        return (totals, (result.astype(jnp.bfloat16), grad_x.astype(jnp.bfloat16)))
    initial = (jnp.zeros(weights.shape, jnp.float32), jnp.zeros(norm_gains.shape, jnp.float32), jnp.zeros(head_gains.shape, jnp.float32))
    totals, seq_outs = lax.scan(per_sequence, initial, (layer_input.reshape(N_DP, SEQ, D), cotangent.reshape(N_DP, SEQ, D), lengths))
    grad_w, grad_g, grad_h = totals
    outputs, input_grads = seq_outs
    new_w, first_w, second_w = adamw(weights, grad_w, moment_weights, square_weights, RATE_WEIGHTS, WEIGHT_DECAY)
    new_g, first_g, second_g = adamw(norm_gains, grad_g, moment_gains, square_gains, RATE_GAINS, 0.0)
    new_h, first_h, second_h = adamw(head_gains, grad_h, moment_head, square_head, RATE_GAINS, 0.0)
    return (outputs.reshape(TOKENS, D), input_grads.reshape(TOKENS, D), new_w, new_g, new_h, first_w, first_g, first_h, second_w, second_g, second_h, new_w.astype(jnp.bfloat16))
```

```python
import numpy as np
import jax
import jax.numpy as jnp
from jax import lax
from jax.sharding import Mesh, PartitionSpec as P

H = 4
HD = 256
FF = 6912
STEP = 10


NORM_EPS = 1e-06
ROPE_BASE = 1000000.0
QUERY_SCALE = 0.0625
BETA_ONE = 0.9
BETA_TWO = 0.95
ADAM_EPS = 1e-08
RATE_WEIGHTS = 0.03
RATE_GAINS = 0.1
WEIGHT_DECAY = 0.1
NEG_LARGE = -1e30

LANES = 128
GROUP = 4
QUARTER = -(-FF // (GROUP * LANES)) * LANES
Q_COLS = H * HD
START_GATE = Q_COLS + 2 * HD
START_OUT = START_GATE + 2 * FF
START_DOWN = START_OUT + Q_COLS
BF = jnp.bfloat16
F32 = jnp.float32


def block_positions(slots, rows, count):
    half_rows = rows // 2
    device = slots // rows
    within = slots % rows
    block = jnp.where(within < half_rows, device, 2 * count - 1 - device)
    return block * half_rows + within % half_rows


def rms_gain(values, gain):
    return values * lax.rsqrt(jnp.mean(values * values, axis=-1, keepdims=True) + NORM_EPS) * gain


def rotate(values, positions):
    half_dim = values.shape[-1] // 2
    freqs = jnp.power(ROPE_BASE, -2.0 * jnp.arange(half_dim).astype(jnp.float32) / values.shape[-1])
    angles = positions.astype(jnp.float32)[:, None] * freqs[None, :]
    cosine = jnp.cos(angles)[:, None, :]
    sine = jnp.sin(angles)[:, None, :]
    first = values[..., :half_dim]
    second = values[..., half_dim:]
    return jnp.concatenate(
        [first * cosine - second * sine, second * cosine + first * sine], axis=-1
    )


def adamw(weight, grad, first, second, rate, decay):
    first_new = BETA_ONE * first + (1.0 - BETA_ONE) * grad
    second_new = BETA_TWO * second + (1.0 - BETA_TWO) * grad * grad
    update = (
        first_new
        / (1.0 - BETA_ONE**STEP)
        / (jnp.sqrt(second_new / (1.0 - BETA_TWO**STEP)) + ADAM_EPS)
    )
    return (weight - rate * (update + decay * weight), first_new, second_new)


def swap(values, axis, distance=1):
    count = lax.axis_size(axis)
    return lax.ppermute(values, axis, [((i + distance) % count, i) for i in range(count)])


def gather_direct(values, axis):
    count, me = lax.axis_size(axis), lax.axis_index(axis)
    out = jnp.zeros((count,) + values.shape, values.dtype)
    out = lax.dynamic_update_index_in_dim(out, values, me, 0)
    for distance in range(1, count):
        got = swap(values, axis, distance)
        out = lax.dynamic_update_index_in_dim(out, got, (me + distance) % count, 0)
    return out


def line_steps(values, axis):
    count = lax.axis_size(axis)
    below, above = [], []
    up, down = values, values
    for step in range(1, count):
        up = lax.ppermute(up, axis, [(i, i + 1) for i in range(step - 1, count - 1)])
        down = lax.ppermute(down, axis, [(i, i - 1) for i in range(1, count - step + 1)])
        below.append(up)
        above.append(down)
    return below, above


def gather_line(values, axis):
    count, me = lax.axis_size(axis), lax.axis_index(axis)
    below, above = line_steps(values, axis)
    out = jnp.zeros((count,) + values.shape, values.dtype)
    out = lax.dynamic_update_index_in_dim(out, values, me, 0)
    for offset in range(1, count):
        got = jnp.where(me + offset < count, above[offset - 1], below[count - offset - 1])
        out = lax.dynamic_update_index_in_dim(out, got, (me + offset) % count, 0)
    return out


def scatter_direct(parts, axis, dim=0):
    count, me = lax.axis_size(axis), lax.axis_index(axis)
    total = lax.dynamic_index_in_dim(parts, me, dim, keepdims=False).astype(F32)
    for distance in range(1, count):
        mine = lax.dynamic_index_in_dim(parts, (me - distance) % count, dim, keepdims=False)
        total = total + swap(mine.astype(BF), axis, distance).astype(F32)
    return total


def scatter_line(parts, axis, dim=0):
    count, me = lax.axis_size(axis), lax.axis_index(axis)

    def own(index):
        return lax.dynamic_index_in_dim(parts, jnp.clip(index, 0, count - 1), dim, keepdims=False)

    up = down = None
    for step in range(1, count):
        far = count - step
        up_out = own(me + far).astype(F32)
        down_out = own(me - far).astype(F32)
        if step > 1:
            up_out, down_out = up_out + up.astype(F32), down_out + down.astype(F32)
        up = lax.ppermute(up_out.astype(BF), axis, [(i, i + 1) for i in range(step)])
        down = lax.ppermute(
            down_out.astype(BF), axis, [(i, i - 1) for i in range(count - step, count)]
        )
    return own(me).astype(F32) + up.astype(F32) + down.astype(F32)


def gather_rows(shard):
    half = shard.shape[1] // 2 // LANES * LANES
    first = gather_direct(shard[:, :half], "x")
    first = gather_direct(gather_line(first, "z"), "r")
    first = gather_direct(first, "c")
    second = gather_direct(shard[:, half:], "r")
    second = gather_direct(gather_line(second, "z"), "x")
    second = gather_direct(second, "c")
    first = first.transpose(1, 2, 3, 0, 4, 5)
    second = second.transpose(3, 2, 1, 0, 4, 5)
    return jnp.concatenate([first, second], axis=-1)


def scatter_rows(parts):
    half = parts.shape[-1] // 2 // LANES * LANES
    first = scatter_direct(parts[..., :half], "c", 3).astype(BF)
    first = scatter_direct(first, "r", 0).astype(BF)
    first = scatter_line(first, "z", 0).astype(BF)
    first = scatter_direct(first, "x", 0)
    second = scatter_direct(parts[..., half:], "c", 3).astype(BF)
    second = scatter_direct(second, "x", 2).astype(BF)
    second = scatter_line(second, "z", 1).astype(BF)
    second = scatter_direct(second, "r", 0)
    return jnp.concatenate([first, second], axis=-1)


def group_permute(values, mask):
    return lax.ppermute(values, ("x", "c"), [(i ^ mask, i) for i in range(GROUP)])


def group_spread(shard):
    rows = shard.shape[0]
    me = 2 * lax.axis_index("x") + lax.axis_index("c")
    out = jnp.zeros((GROUP, rows, QUARTER), shard.dtype)
    for mask in range(GROUP):
        mine = lax.dynamic_slice_in_dim(shard, (me ^ mask) * QUARTER, QUARTER, 1)
        got = group_permute(mine, mask) if mask else mine
        out = lax.dynamic_update_index_in_dim(out, got, me ^ mask, 0)
    return out.reshape(GROUP * rows, QUARTER)


def group_collect(block):
    rows = block.shape[0] // GROUP
    me = 2 * lax.axis_index("x") + lax.axis_index("c")
    parts = block.reshape(GROUP, rows, QUARTER)
    out = jnp.zeros((rows, GROUP * QUARTER), block.dtype)
    for mask in range(GROUP):
        mine = lax.dynamic_index_in_dim(parts, me ^ mask, 0, keepdims=False)
        got = group_permute(mine, mask) if mask else mine
        out = lax.dynamic_update_slice_in_dim(out, got, (me ^ mask) * QUARTER, 1)
    return out


def gather_blocks(block):
    full = gather_direct(gather_line(block, "z"), "r")
    return full.reshape(-1, block.shape[1])


def scatter_blocks(parts):
    r_count, z_count = lax.axis_size("r"), lax.axis_size("z")
    parts = parts.reshape(r_count, z_count, -1, parts.shape[1])
    return scatter_line(scatter_direct(parts, "r", 0).astype(BF), "z", 0)


def exchange(values):
    other = swap(values, "c")
    across = swap(values, "x")
    across_other = swap(across, "c")
    return jnp.concatenate([values, other, across, across_other], axis=0)


def exchange_back(parts):
    rows = parts.shape[0] // GROUP
    own, other, across, across_other = (parts[i * rows : (i + 1) * rows] for i in range(GROUP))
    far = across + swap(across_other.astype(BF), "c").astype(F32)
    near = own + swap(other.astype(BF), "c").astype(F32)
    return near + swap(far.astype(BF), "x").astype(F32)


def pad_cols(values, cols):
    return jnp.pad(values, ((0, 0), (0, cols - values.shape[1])))


def body(
    layer_input,
    cotangent,
    lengths,
    weights,
    norm_gains,
    head_gains,
    moment_weights,
    moment_gains,
    moment_head,
    square_weights,
    square_gains,
    square_head,
):
    rows = weights.shape[0]
    head_rows = head_gains.shape[0]
    width = layer_input.shape[1]
    r_count, z_count = lax.axis_size("r"), lax.axis_size("z")

    weights_low = weights.astype(BF)
    gain_cols = jnp.zeros((max(rows, head_rows), LANES), BF)
    gain_cols = gain_cols.at[:rows, :4].set(norm_gains.astype(BF))
    gain_cols = gain_cols.at[:head_rows, 4:6].set(head_gains.astype(BF))[:rows]
    first_shard = jnp.concatenate([weights_low[:, :START_GATE], gain_cols], axis=1)
    first_full = gather_rows(first_shard)
    w_qkv = first_full[..., :START_GATE].reshape(width, START_GATE)
    gain_part = first_full[..., START_GATE:]
    gain_f = 1.0 + gain_part[..., :4].reshape(width, 4).astype(F32)
    head_f = (
        gain_part[..., :head_rows, 4:6].transpose(0, 2, 3, 1, 4, 5).reshape(HD, 2).astype(F32)
    ) + 1.0
    w_out = gather_rows(weights_low[:, START_OUT:START_DOWN]).reshape(width, Q_COLS)
    padded = GROUP * QUARTER
    w_gate = gather_blocks(group_spread(pad_cols(weights_low[:, START_GATE : START_GATE + FF], padded)))
    w_up = gather_blocks(group_spread(pad_cols(weights_low[:, START_GATE + FF : START_OUT], padded)))
    w_down = gather_blocks(group_spread(pad_cols(weights_low[:, START_DOWN:], padded)))

    order = (
        np.arange(width)
        .reshape(r_count, 2, 2, z_count, rows)
        .transpose(0, 3, 1, 2, 4)
        .reshape(width)
    )
    place = (jnp.arange(width)[:, None] == jnp.asarray(order)[None, :]).astype(BF)

    tok_rows = layer_input.shape[0]
    ctx_count = z_count
    local_slots = lax.axis_index("z") * tok_rows + jnp.arange(tok_rows, dtype=jnp.int32)
    positions = block_positions(local_slots, tok_rows, ctx_count)
    seq_length = lengths[0]
    row_valid = positions < seq_length
    inputs = jnp.dot(layer_input, place, preferred_element_type=F32)
    cot = jnp.dot(cotangent, place, preferred_element_type=F32)
    normed_in, pull_in = jax.vjp(rms_gain, inputs, gain_f[:, 0])
    normed_low = normed_in.astype(BF)
    projected = jnp.dot(normed_low, w_qkv, preferred_element_type=F32)

    def query_key(query_raw, key_raw, head_arg):
        query_out = (
            rotate(rms_gain(query_raw.reshape(tok_rows, H, HD), head_arg[:, 0]), positions)
            * QUERY_SCALE
        )
        key_out = rotate(rms_gain(key_raw[:, None, :], head_arg[:, 1]), positions)[:, 0]
        return (query_out, key_out)

    (queries, keys), pull_qk = jax.vjp(
        query_key, projected[:, :Q_COLS], projected[:, Q_COLS : Q_COLS + HD], head_f
    )
    query_low = queries.astype(BF)
    key_low = keys.astype(BF)
    value_low = projected[:, Q_COLS + HD :].astype(BF)
    key_value = gather_line(jnp.concatenate([key_low, value_low], axis=1), "z")
    key_value = key_value.reshape(z_count * tok_rows, 2 * HD)
    all_keys, all_values = key_value[:, :HD], key_value[:, HD:]
    key_pos = block_positions(jnp.arange(all_keys.shape[0], dtype=jnp.int32), tok_rows, ctx_count)
    allowed = (key_pos[None, :] <= positions[:, None]) & (key_pos < seq_length)[None, :]
    scores = jnp.einsum("thd,sd->hts", query_low, all_keys, preferred_element_type=F32)
    scores = jnp.where(allowed[None], scores, NEG_LARGE)
    row_max = jnp.max(scores, axis=-1, keepdims=True)
    expon = jnp.exp(scores - row_max)
    row_total = jnp.sum(expon, axis=-1, keepdims=True)
    probs_low = (expon / row_total).astype(BF)
    log_total = (row_max + jnp.log(row_total))[..., 0]
    mixed = jnp.einsum("hts,sd->thd", probs_low, all_values, preferred_element_type=F32)
    mixed_low = mixed.reshape(tok_rows, Q_COLS).astype(BF)
    attn_proj = jnp.einsum("tc,dc->td", mixed_low, w_out, preferred_element_type=F32)
    post_attn, pull_attn = jax.vjp(rms_gain, attn_proj, gain_f[:, 1])
    residual_mid = inputs + post_attn
    normed_mid, pull_mid = jax.vjp(rms_gain, residual_mid, gain_f[:, 2])

    mid_low = exchange(normed_mid.astype(BF))
    gate = jnp.dot(mid_low, w_gate, preferred_element_type=F32)
    up = jnp.dot(mid_low, w_up, preferred_element_type=F32)

    def geglu(gate_arg, up_arg):
        return jax.nn.gelu(gate_arg, approximate=True) * up_arg

    hidden, pull_hidden = jax.vjp(geglu, gate, up)
    hidden_low = hidden.astype(BF)
    mlp_part = jnp.einsum("tf,df->td", hidden_low, w_down, preferred_element_type=F32)
    mlp_proj = exchange_back(mlp_part)
    post_mlp, pull_mlp = jax.vjp(rms_gain, mlp_proj, gain_f[:, 3])
    output_low = (residual_mid + post_mlp).astype(BF)
    out_grad = cot * row_valid[:, None].astype(F32)
    mlp_grad, grad_three = pull_mlp(out_grad)
    mlp_grad_low = exchange(mlp_grad.astype(BF))
    hidden_grad = jnp.dot(mlp_grad_low, w_down, preferred_element_type=F32)
    gate_grad, up_grad = pull_hidden(hidden_grad)
    gate_low, up_low = gate_grad.astype(BF), up_grad.astype(BF)
    mid_part = jnp.einsum("tc,dc->td", gate_low, w_gate, preferred_element_type=F32)
    mid_part += jnp.einsum("tc,dc->td", up_low, w_up, preferred_element_type=F32)
    mid_grad = exchange_back(mid_part)
    grad_down = jnp.einsum("td,tf->df", mlp_grad_low, hidden_low, preferred_element_type=F32)
    grad_gate = jnp.einsum("td,tf->df", mid_low, gate_low, preferred_element_type=F32)
    grad_up = jnp.einsum("td,tf->df", mid_low, up_low, preferred_element_type=F32)
    sum_down = group_collect(scatter_blocks(grad_down.astype(BF)).astype(BF))[:, :FF]
    sum_gate = group_collect(scatter_blocks(grad_gate.astype(BF)).astype(BF))[:, :FF]
    sum_up = group_collect(scatter_blocks(grad_up.astype(BF)).astype(BF))[:, :FF]

    resid_part, grad_two = pull_mid(mid_grad)
    residual_grad = out_grad + resid_part
    attn_grad, grad_one = pull_attn(residual_grad)
    attn_low = attn_grad.astype(BF)
    grad_out = jnp.einsum("td,tc->dc", attn_low, mixed_low, preferred_element_type=F32)
    row_shape = (r_count, z_count, 2, 2, rows)
    sum_out = scatter_rows(grad_out.astype(BF).reshape(row_shape + (Q_COLS,)))
    mixed_grad = jnp.dot(attn_low, w_out, preferred_element_type=F32).astype(BF)
    query_heads = query_low.transpose(1, 0, 2)
    grad_heads = mixed_grad.reshape(tok_rows, H, HD).transpose(1, 0, 2)

    def head_back(head_in):
        query_one, grad_one_head, total_one = head_in
        head_scores = jnp.einsum("td,sd->ts", query_one, all_keys, preferred_element_type=F32)
        head_scores = jnp.where(allowed, head_scores, NEG_LARGE)
        head_probs = jnp.exp(head_scores - total_one[:, None])
        prob_grad = jnp.einsum("td,sd->ts", grad_one_head, all_values, preferred_element_type=F32)
        delta_row = jnp.sum(head_probs * prob_grad, axis=-1, keepdims=True)
        score_low = (head_probs * (prob_grad - delta_row)).astype(BF)
        query_grad = jnp.dot(score_low, all_keys, preferred_element_type=F32)
        key_part = jnp.einsum("ts,td->sd", score_low, query_one, preferred_element_type=F32)
        value_part = jnp.einsum(
            "ts,td->sd", head_probs.astype(BF), grad_one_head, preferred_element_type=F32
        )
        return (query_grad, key_part, value_part)

    query_grads, key_parts, value_parts = lax.map(head_back, (query_heads, grad_heads, log_total))
    key_value_part = jnp.concatenate(
        [jnp.sum(key_parts, axis=0), jnp.sum(value_parts, axis=0)], axis=1
    )
    key_value_grad = scatter_line(
        key_value_part.astype(BF).reshape(z_count, tok_rows, 2 * HD), "z", 0
    )
    raw_query, raw_key, grad_head = pull_qk(
        (query_grads.transpose(1, 0, 2), key_value_grad[:, :HD])
    )
    proj_low = jnp.concatenate([raw_query, raw_key, key_value_grad[:, HD:]], axis=1).astype(BF)
    grad_qkv = jnp.einsum("td,tc->dc", normed_low, proj_low, preferred_element_type=F32)
    in_part = jnp.einsum("tc,dc->td", proj_low, w_qkv, preferred_element_type=F32)
    input_part, grad_zero = pull_in(in_part)
    grad_input_low = (residual_grad + input_part).astype(BF)

    gain_grads = jnp.stack([grad_zero, grad_one, grad_two, grad_three], axis=1)
    gain_grads = gain_grads.reshape(row_shape + (4,))
    head_grads = grad_head.reshape(r_count, 2, 2, z_count, head_rows, 2).transpose(0, 3, 1, 2, 4, 5)
    side = jnp.zeros((r_count, z_count, 2, 2, rows, LANES), BF)
    side = side.at[..., :4].set(gain_grads.astype(BF))
    side = side.at[..., :head_rows, 4:6].set(head_grads.astype(BF))
    qkv_parts = jnp.concatenate(
        [grad_qkv.astype(BF).reshape(row_shape + (START_GATE,)), side], axis=-1
    )
    sum_first = scatter_rows(qkv_parts)
    sum_qkv = sum_first[:, :START_GATE]
    sum_gains = sum_first[:, START_GATE : START_GATE + 4]
    sum_head = sum_first[:head_rows, START_GATE + 4 : START_GATE + 6]

    output = lax.dot_general(
        output_low, place, (((1,), (1,)), ((), ())), preferred_element_type=F32
    ).astype(BF)
    grad_input = lax.dot_general(
        grad_input_low, place, (((1,), (1,)), ((), ())), preferred_element_type=F32
    ).astype(BF)

    sum_weights = jnp.concatenate(
        [sum_qkv, sum_gate.astype(F32), sum_up.astype(F32), sum_out, sum_down.astype(F32)], axis=1
    )
    new_w, first_w, second_w = adamw(
        weights, sum_weights, moment_weights, square_weights, RATE_WEIGHTS, WEIGHT_DECAY
    )
    new_g, first_g, second_g = adamw(
        norm_gains, sum_gains, moment_gains, square_gains, RATE_GAINS, 0.0
    )
    new_h, first_h, second_h = adamw(
        head_gains, sum_head, moment_head, square_head, RATE_GAINS, 0.0
    )
    return (
        output,
        grad_input,
        new_w,
        new_g,
        new_h,
        first_w,
        first_g,
        first_h,
        second_w,
        second_g,
        second_h,
        new_w.astype(BF),
    )


def solution(mesh):
    dp_count, ctx_count = mesh.shape["dp"], mesh.shape["ctx"]
    inner = Mesh(mesh.devices.reshape(dp_count // 4, 2, 2, ctx_count), ("r", "x", "c", "z"))
    rows = P(("r", "x", "c", "z"), None)
    in_specs = (rows, rows, P(("r", "x", "c"))) + (rows,) * 9
    return jax.shard_map(
        body, mesh=inner, in_specs=in_specs, out_specs=(rows,) * 12, check_vma=False
    )
```

```python
import numpy as np
import jax
import jax.numpy as jnp
from jax import lax
from jax.experimental import pallas as pl
from jax.experimental.pallas import tpu as pltpu
from jax.sharding import PartitionSpec as P

H = 4
HD = 256
FF = 6912
STEP = 10


NORM_EPS = 1e-06
ROPE_BASE = 1000000.0
QUERY_SCALE = 0.0625
BETA_ONE = 0.9
BETA_TWO = 0.95
ADAM_EPS = 1e-08
RATE_WEIGHTS = 0.03
RATE_GAINS = 0.1
WEIGHT_DECAY = 0.1
NEG_LARGE = -1e30

LANES = 128
Q_COLS = H * HD
START_GATE = Q_COLS + 2 * HD
START_OUT = START_GATE + 2 * FF
START_DOWN = START_OUT + Q_COLS
BF = jnp.bfloat16
F32 = jnp.float32


def block_positions(slots, rows, count):
    half_rows = rows // 2
    device = slots // rows
    within = slots % rows
    block = jnp.where(within < half_rows, device, 2 * count - 1 - device)
    return block * half_rows + within % half_rows


def rms_gain(values, gain):
    return values * lax.rsqrt(jnp.mean(values * values, axis=-1, keepdims=True) + NORM_EPS) * gain


def rotate(values, positions):
    half_dim = values.shape[-1] // 2
    freqs = jnp.power(ROPE_BASE, -2.0 * jnp.arange(half_dim).astype(jnp.float32) / values.shape[-1])
    angles = positions.astype(jnp.float32)[:, None] * freqs[None, :]
    cosine = jnp.cos(angles)[:, None, :]
    sine = jnp.sin(angles)[:, None, :]
    first = values[..., :half_dim]
    second = values[..., half_dim:]
    return jnp.concatenate(
        [first * cosine - second * sine, second * cosine + first * sine], axis=-1
    )


def adamw(weight, grad, first, second, rate, decay):
    first_new = BETA_ONE * first + (1.0 - BETA_ONE) * grad
    second_new = BETA_TWO * second + (1.0 - BETA_TWO) * grad * grad
    update = (
        first_new
        / (1.0 - BETA_ONE**STEP)
        / (jnp.sqrt(second_new / (1.0 - BETA_TWO**STEP)) + ADAM_EPS)
    )
    return (weight - rate * (update + decay * weight), first_new, second_new)


def shift(values, axis, distance):
    count = lax.axis_size(axis)
    return lax.ppermute(values, axis, [((i + distance) % count, i) for i in range(count)])


def flip(values, bit):
    return lax.ppermute(values, "dp", [(i ^ bit, i) for i in range(lax.axis_size("dp"))])


def my_bit(bit):
    return (lax.axis_index("dp") // bit) % 2


def chip_orders():
    bits = [1 << i for i in range(1, lax.axis_size("dp").bit_length() - 1)]
    return bits, bits[::-1]


def bit_orders():
    return tuple(bits + [1] for bits in chip_orders())


def place_blocks(blocks, axis):
    count, me = len(blocks), lax.axis_index(axis)
    return jnp.stack([lax.select_n((j - me) % count, *blocks) for j in range(count)])


def gather_direct(values, axis):
    count = lax.axis_size(axis)
    blocks = [values] + [shift(values, axis, distance) for distance in range(1, count)]
    return place_blocks(blocks, axis)


def gather_line(values, axis):
    count, me = lax.axis_size(axis), lax.axis_index(axis)
    below, above = [], []
    up, down = values, values
    for step in range(1, count):
        up = lax.ppermute(up, axis, [(i, i + 1) for i in range(step - 1, count - 1)])
        down = lax.ppermute(down, axis, [(i, i - 1) for i in range(1, count - step + 1)])
        below.append(up)
        above.append(down)
    blocks = [values]
    for offset in range(1, count):
        blocks.append(
            jnp.where(me + offset < count, above[offset - 1], below[count - offset - 1])
        )
    return place_blocks(blocks, axis)


def scatter_direct(parts, axis):
    count, me = lax.axis_size(axis), lax.axis_index(axis)
    total = lax.dynamic_index_in_dim(parts, me, 0, keepdims=False).astype(F32)
    for distance in range(1, count):
        mine = lax.dynamic_index_in_dim(parts, (me - distance) % count, 0, keepdims=False)
        total = total + shift(mine.astype(BF), axis, distance).astype(F32)
    return total


def scatter_line(parts, axis):
    count, me = lax.axis_size(axis), lax.axis_index(axis)

    def own(index):
        return lax.dynamic_index_in_dim(parts, jnp.clip(index, 0, count - 1), 0, keepdims=False)

    up = down = None
    for step in range(1, count):
        far = count - step
        up_out = own(me + far).astype(F32)
        down_out = own(me - far).astype(F32)
        if step > 1:
            up_out, down_out = up_out + up.astype(F32), down_out + down.astype(F32)
        up = lax.ppermute(up_out.astype(BF), axis, [(i, i + 1) for i in range(step)])
        down = lax.ppermute(
            down_out.astype(BF), axis, [(i, i - 1) for i in range(count - step, count)]
        )
    return own(me).astype(F32) + up.astype(F32) + down.astype(F32)


def split_cols(cols):
    half = cols // 2 // LANES * LANES
    return ((0, half), (half, cols))


def gather_rows(shard):
    rows, cols = shard.shape
    z_block = gather_direct(shard, "ctx")
    z_count = z_block.shape[0]
    halves = []
    for (low, high), bits in zip(split_cols(cols), bit_orders()):
        part = z_block[..., low:high]
        for bit in bits:
            got, mine = flip(part, bit), my_bit(bit)
            part = jnp.stack([jnp.where(mine == 0, part, got), jnp.where(mine == 0, got, part)])
        axes = bits[::-1]
        order = [axes.index(bit) for bit in sorted(bits, reverse=True)]
        count = len(bits)
        part = part.transpose([count] + order + [count + 1, count + 2])
        halves.append(part.reshape(z_count, -1, rows, high - low))
    return jnp.concatenate(halves, axis=-1).reshape(-1, cols)


def scatter_rows(parts):
    z_count, dp_count, rows, cols = parts.shape
    halves = []
    for (low, high), bits in zip(split_cols(cols), bit_orders()):
        part = parts[..., low:high]
        part = part.reshape((z_count,) + (2,) * len(bits) + (rows, high - low))
        left = sorted(bits, reverse=True)
        for bit in bits[::-1]:
            dim, mine = 1 + left.index(bit), my_bit(bit)
            keep = lax.dynamic_index_in_dim(part, mine, dim, keepdims=False)
            send = lax.dynamic_index_in_dim(part, 1 - mine, dim, keepdims=False)
            part = (keep.astype(F32) + flip(send, bit).astype(F32)).astype(BF)
            left.remove(bit)
        halves.append(part)
    return scatter_direct(jnp.concatenate(halves, axis=-1), "ctx")


def spread(values):
    half = values.shape[0] // 2
    out = []
    for part, bits in zip((values[:half], values[half:]), chip_orders()):
        for bit in bits:
            part = jnp.concatenate([part, flip(part, bit)], axis=0)
        out.append(part)
    return jnp.concatenate(out, axis=0)


def collect(parts):
    half = parts.shape[0] // 2
    out = []
    for part, bits in zip((parts[:half], parts[half:]), chip_orders()):
        for bit in bits[::-1]:
            count = part.shape[0] // 2
            got = flip(part[count:].astype(BF), bit)
            part = part[:count].astype(F32) + got.astype(F32)
        out.append(part)
    return jnp.concatenate(out, axis=0)


def pad_cols(values, cols):
    return jnp.pad(values, ((0, 0), (0, cols - values.shape[1])))


VMEM_LIMIT = 60 * 1024 * 1024
NT = (((1,), (1,)), ((), ()))
TN = (((0,), (0,)), ((), ()))


def dot(left, right, dims=(((1,), (0,)), ((), ()))):
    return lax.dot_general(left, right, dims, preferred_element_type=F32)


def whole(shape):
    return pl.BlockSpec(shape, lambda i: (0,) * len(shape))


def tie_kernel(value_ref, other_ref, out_ref):
    del value_ref, other_ref, out_ref


def tie(value, other):
    return pl.pallas_call(
        tie_kernel,
        out_shape=jax.ShapeDtypeStruct(value.shape, value.dtype),
        in_specs=[pl.BlockSpec(memory_space=pl.ANY)] * 2,
        out_specs=pl.BlockSpec(memory_space=pl.ANY),
        input_output_aliases={0: 0},
        compiler_params=pltpu.CompilerParams(has_side_effects=True),
    )(value, other)


def key_row(block, rows, count):
    first = block * 2 * rows
    second = (2 * count - 1 - block) * 2 * rows + rows
    return pl.multiple_of(jnp.where(block < count, first, second), rows)


def key_bias(block, rows, length):
    spots = block * rows + lax.broadcasted_iota(jnp.int32, (1, rows), 1)
    return jnp.where(spots < length, 0.0, NEG_LARGE)


def attend_kernel(info_ref, query_ref, kv_ref, mixed_ref, total_ref, acc_ref, sum_ref):
    rows = query_ref.shape[0]
    count = kv_ref.shape[0] // (2 * rows)
    place, length = info_ref[0], info_ref[1]
    mine = jnp.where(pl.program_id(0) == 0, place, 2 * count - 1 - place)
    acc_ref[...] = jnp.zeros_like(acc_ref)
    sum_ref[...] = jnp.zeros_like(sum_ref)

    def step(block, causal):
        at = pl.ds(key_row(block, rows, count), rows)
        keys, values = kv_ref[at, :HD], kv_ref[at, HD:]
        bias = key_bias(block, rows, length)
        for head in range(H):
            cols = slice(head * HD, (head + 1) * HD)
            scores = dot(query_ref[:, cols], keys, NT) + bias
            weight = jnp.exp(scores)
            if causal:
                row = lax.broadcasted_iota(jnp.int32, (rows, rows), 0)
                col = lax.broadcasted_iota(jnp.int32, (rows, rows), 1)
                weight = jnp.where(col <= row, weight, 0.0)
            parts = weight[:, :LANES]
            for low in range(LANES, rows, LANES):
                parts = parts + weight[:, low : low + LANES]
            sum_ref[:, head * LANES : (head + 1) * LANES] += parts
            acc_ref[:, cols] += dot(weight.astype(BF), values)

    def loop(block, carry):
        step(block, False)
        return carry

    lax.fori_loop(0, mine, loop, 0)
    step(mine, True)
    for head in range(H):
        cols = slice(head * HD, (head + 1) * HD)
        total = jnp.sum(sum_ref[:, head * LANES : (head + 1) * LANES], axis=1, keepdims=True)
        inverse = 1.0 / total
        mixed_ref[:, cols] = (acc_ref[:, cols] * inverse).astype(BF)
        total_ref[:, head * LANES : (head + 1) * LANES] = jnp.broadcast_to(
            inverse, (rows, LANES)
        )


def attend(info, query, kv):
    half = query.shape[0] // 2
    spec = lambda cols: pl.BlockSpec((half, cols), lambda i, info: (i, 0))
    return pl.pallas_call(
        attend_kernel,
        grid_spec=pltpu.PrefetchScalarGridSpec(
            num_scalar_prefetch=1,
            grid=(2,),
            in_specs=[spec(Q_COLS), pl.BlockSpec(kv.shape, lambda i, info: (0, 0))],
            out_specs=[spec(Q_COLS), spec(H * LANES)],
            scratch_shapes=[pltpu.VMEM((half, Q_COLS), F32), pltpu.VMEM((half, H * LANES), F32)],
        ),
        out_shape=[
            jax.ShapeDtypeStruct((2 * half, Q_COLS), BF),
            jax.ShapeDtypeStruct((2 * half, H * LANES), F32),
        ],
        compiler_params=pltpu.CompilerParams(vmem_limit_bytes=VMEM_LIMIT),
        cost_estimate=pl.CostEstimate(
            flops=4 * half * half * Q_COLS * 9, bytes_accessed=8 << 20, transcendentals=0
        ),
    )(info, query, kv)


def attend_back_kernel(
    info_ref, query_ref, grad_ref, mixed_ref, total_ref, kv_ref, dq_ref, dkv_ref, acc_ref, dq_acc
):
    rows = query_ref.shape[0]
    count = kv_ref.shape[0] // (2 * rows)
    place, length = info_ref[0], info_ref[1]
    step_id = pl.program_id(0)
    mine = jnp.where(step_id == 0, place, 2 * count - 1 - place)

    @pl.when(step_id == 0)
    def _():
        acc_ref[...] = jnp.zeros_like(acc_ref)

    dq_acc[...] = jnp.zeros_like(dq_acc)
    delta, inverse = [], []
    for head in range(H):
        cols = slice(head * HD, (head + 1) * HD)
        delta.append(
            jnp.sum(
                grad_ref[:, cols].astype(F32) * mixed_ref[:, cols].astype(F32),
                axis=1,
                keepdims=True,
            )
        )
        inverse.append(total_ref[:, head * LANES : head * LANES + 1])

    def step(block, causal):
        at = pl.ds(key_row(block, rows, count), rows)
        keys, values = kv_ref[at, :HD], kv_ref[at, HD:]
        bias = key_bias(block, rows, length)
        dk = jnp.zeros((rows, HD), F32)
        dv = jnp.zeros((rows, HD), F32)
        for head in range(H):
            cols = slice(head * HD, (head + 1) * HD)
            query, grad = query_ref[:, cols], grad_ref[:, cols]
            weight = jnp.exp(dot(query, keys, NT) + bias) * inverse[head]
            if causal:
                row = lax.broadcasted_iota(jnp.int32, (rows, rows), 0)
                col = lax.broadcasted_iota(jnp.int32, (rows, rows), 1)
                weight = jnp.where(col <= row, weight, 0.0)
            score = (weight * (dot(grad, values, NT) - delta[head])).astype(BF)
            dq_acc[:, cols] += dot(score, keys)
            dk = dk + dot(score, query, TN)
            dv = dv + dot(weight.astype(BF), grad, TN)
        acc_ref[at, :HD] += dk
        acc_ref[at, HD:] += dv

    def loop(block, carry):
        step(block, False)
        return carry

    lax.fori_loop(0, mine, loop, 0)
    step(mine, True)
    dq_ref[...] = dq_acc[...]

    @pl.when(step_id == pl.num_programs(0) - 1)
    def _():
        dkv_ref[...] = acc_ref[...].astype(BF)


def attend_back(info, query, grad, mixed, total, kv):
    half = query.shape[0] // 2
    spec = lambda cols: pl.BlockSpec((half, cols), lambda i, info: (i, 0))
    full = pl.BlockSpec(kv.shape, lambda i, info: (0, 0))
    return pl.pallas_call(
        attend_back_kernel,
        grid_spec=pltpu.PrefetchScalarGridSpec(
            num_scalar_prefetch=1,
            grid=(2,),
            in_specs=[spec(Q_COLS), spec(Q_COLS), spec(Q_COLS), spec(H * LANES), full],
            out_specs=[spec(Q_COLS), full],
            scratch_shapes=[pltpu.VMEM(kv.shape, F32), pltpu.VMEM((half, Q_COLS), F32)],
        ),
        out_shape=[
            jax.ShapeDtypeStruct((2 * half, Q_COLS), F32),
            jax.ShapeDtypeStruct(kv.shape, BF),
        ],
        compiler_params=pltpu.CompilerParams(vmem_limit_bytes=VMEM_LIMIT),
        cost_estimate=pl.CostEstimate(
            flops=10 * half * half * Q_COLS * 9, bytes_accessed=12 << 20, transcendentals=0
        ),
    )(info, query, grad, mixed, total, kv)


GELU_A = 0.7978845608028654
GELU_B = 0.044715


def mlp_kernel(x_ref, own_ref, other_ref, part_ref, gate_up_ref, hidden_ref):
    units = own_ref.shape[1] // 3
    total = None
    for k, w_ref in enumerate((own_ref, other_ref)):
        both = dot(x_ref[...], w_ref[:, : 2 * units])
        gate_up_ref[:, k * 2 * units : (k + 1) * 2 * units] = both.astype(BF)
        gate, up = both[:, :units], both[:, units:]
        inner = jnp.tanh(GELU_A * gate * (1.0 + GELU_B * gate * gate))
        hidden = (0.5 * gate * (1.0 + inner) * up).astype(BF)
        hidden_ref[:, k * units : (k + 1) * units] = hidden
        part = dot(hidden, w_ref[:, 2 * units :], NT)
        total = part if total is None else total + part
    part_ref[...] = total.astype(BF)


def mlp_tile(rows):
    return min(rows, 512)


def mlp_forward(x, own, other):
    rows, width = x.shape
    units = own.shape[1] // 3
    tile = mlp_tile(rows)
    spec = lambda cols: pl.BlockSpec((tile, cols), lambda i: (i, 0))
    return pl.pallas_call(
        mlp_kernel,
        grid=(rows // tile,),
        in_specs=[spec(width), whole(own.shape), whole(own.shape)],
        out_specs=[spec(width), spec(4 * units), spec(2 * units)],
        out_shape=[
            jax.ShapeDtypeStruct((rows, width), BF),
            jax.ShapeDtypeStruct((rows, 4 * units), BF),
            jax.ShapeDtypeStruct((rows, 2 * units), BF),
        ],
        compiler_params=pltpu.CompilerParams(vmem_limit_bytes=VMEM_LIMIT),
        cost_estimate=pl.CostEstimate(
            flops=12 * rows * width * units, bytes_accessed=32 << 20, transcendentals=0
        ),
    )(x, own, other)


def mlp_back_kernel(grad_ref, gate_up_ref, own_ref, other_ref, part_ref, gate_up_grad_ref):
    units = own_ref.shape[1] // 3
    total = None
    for k, w_ref in enumerate((own_ref, other_ref)):
        base = k * 2 * units
        hidden_grad = dot(grad_ref[...], w_ref[:, 2 * units :])
        gate = gate_up_ref[:, base : base + units].astype(F32)
        up = gate_up_ref[:, base + units : base + 2 * units].astype(F32)
        square = gate * gate
        inner = jnp.tanh(GELU_A * gate * (1.0 + GELU_B * square))
        half = 0.5 * (1.0 + inner)
        slope = half + 0.5 * gate * (1.0 - inner * inner) * (
            GELU_A * (1.0 + 3.0 * GELU_B * square)
        )
        gate_grad = (hidden_grad * up * slope).astype(BF)
        up_grad = (hidden_grad * (gate * half)).astype(BF)
        gate_up_grad_ref[:, base : base + units] = gate_grad
        gate_up_grad_ref[:, base + units : base + 2 * units] = up_grad
        part = dot(gate_up_grad_ref[:, base : base + 2 * units], w_ref[:, : 2 * units], NT)
        total = part if total is None else total + part
    part_ref[...] = total.astype(BF)


def mlp_backward(grad, gate_up, own, other):
    rows, width = grad.shape
    units = own.shape[1] // 3
    tile = mlp_tile(rows)
    spec = lambda cols: pl.BlockSpec((tile, cols), lambda i: (i, 0))
    return pl.pallas_call(
        mlp_back_kernel,
        grid=(rows // tile,),
        in_specs=[spec(width), spec(4 * units), whole(own.shape), whole(own.shape)],
        out_specs=[spec(width), spec(4 * units)],
        out_shape=[
            jax.ShapeDtypeStruct((rows, width), BF),
            jax.ShapeDtypeStruct((rows, 4 * units), BF),
        ],
        compiler_params=pltpu.CompilerParams(vmem_limit_bytes=VMEM_LIMIT),
        cost_estimate=pl.CostEstimate(
            flops=12 * rows * width * units, bytes_accessed=32 << 20, transcendentals=0
        ),
    )(grad, gate_up, own, other)


def body(
    layer_input,
    cotangent,
    lengths,
    weights,
    norm_gains,
    head_gains,
    moment_weights,
    moment_gains,
    moment_head,
    square_weights,
    square_gains,
    square_head,
):
    rows = weights.shape[0]
    head_rows = head_gains.shape[0]
    width = layer_input.shape[1]
    dp_count, z_count = lax.axis_size("dp"), lax.axis_size("ctx")
    units = -(-FF // (dp_count * LANES)) * LANES

    weights_low = weights.astype(BF)
    gain_cols = jnp.zeros((max(rows, head_rows), LANES), BF)
    gain_cols = gain_cols.at[:rows, :4].set(norm_gains.astype(BF))
    gain_cols = gain_cols.at[:head_rows, 4:6].set(head_gains.astype(BF))[:rows]
    first_shard = jnp.concatenate([weights_low[:, :START_GATE], gain_cols], axis=1)
    mlp_shard = jnp.concatenate(
        [
            pad_cols(weights_low[:, start : start + FF], dp_count * units)
            .reshape(rows, dp_count, units)
            .transpose(1, 0, 2)
            for start in (START_GATE, START_GATE + FF, START_DOWN)
        ],
        axis=2,
    )
    mlp_block = lax.all_to_all(mlp_shard, "dp", split_axis=0, concat_axis=0, tiled=True)
    mlp_block = mlp_block.reshape(dp_count * rows, 3 * units)
    w_own = lax.all_gather(mlp_block, "ctx", axis=0, tiled=True)
    w_other = flip(w_own, 1)
    first_full = gather_rows(first_shard)
    w_qkv = first_full[:, :START_GATE]
    gain_part = first_full[:, START_GATE:].astype(F32)
    gain_f = 1.0 + gain_part[:, :4]
    head_f = gain_part.reshape(z_count, dp_count, rows, LANES)[:, :, :head_rows, 4:6]
    head_f = 1.0 + head_f.transpose(1, 0, 2, 3).reshape(HD, 2)
    w_out = gather_rows(tie(weights_low[:, START_OUT:START_DOWN], first_full))

    order = np.arange(width).reshape(dp_count, z_count, rows).transpose(1, 0, 2).reshape(width)
    place = (jnp.arange(width)[:, None] == jnp.asarray(order)[None, :]).astype(BF)

    tok_rows = layer_input.shape[0]
    ctx_count = z_count
    local_slots = lax.axis_index("ctx") * tok_rows + jnp.arange(tok_rows, dtype=jnp.int32)
    positions = block_positions(local_slots, tok_rows, ctx_count)
    seq_length = lengths[0]
    row_valid = positions < seq_length
    inputs = jnp.dot(layer_input, place, preferred_element_type=F32)
    cot = jnp.dot(cotangent, place, preferred_element_type=F32)
    normed_in, pull_in = jax.vjp(rms_gain, inputs, gain_f[:, 0])
    normed_low = normed_in.astype(BF)
    projected = jnp.dot(normed_low, w_qkv, preferred_element_type=F32)

    def query_key(query_raw, key_raw, head_arg):
        query_out = (
            rotate(rms_gain(query_raw.reshape(tok_rows, H, HD), head_arg[:, 0]), positions)
            * QUERY_SCALE
        )
        key_out = rotate(rms_gain(key_raw[:, None, :], head_arg[:, 1]), positions)[:, 0]
        return (query_out, key_out)

    (queries, keys), pull_qk = jax.vjp(
        query_key, projected[:, :Q_COLS], projected[:, Q_COLS : Q_COLS + HD], head_f
    )
    query_low = queries.astype(BF)
    key_low = keys.astype(BF)
    value_low = projected[:, Q_COLS + HD :].astype(BF)
    key_value = gather_line(jnp.concatenate([key_low, value_low], axis=1), "ctx")
    key_value = key_value.reshape(z_count * tok_rows, 2 * HD)
    info = jnp.stack([lax.axis_index("ctx"), seq_length]).astype(jnp.int32)
    query_low = query_low.reshape(tok_rows, Q_COLS)
    mixed_low, inverse_total = attend(info, query_low, key_value)
    attn_proj = jnp.einsum("tc,dc->td", mixed_low, w_out, preferred_element_type=F32)
    post_attn, pull_attn = jax.vjp(rms_gain, attn_proj, gain_f[:, 1])
    residual_mid = inputs + post_attn
    normed_mid, pull_mid = jax.vjp(rms_gain, residual_mid, gain_f[:, 2])

    mid_low = normed_mid.astype(BF)
    out_grad = cot * row_valid[:, None].astype(F32)
    chunks = 2
    size = tok_rows // chunks
    spans = [slice(i * size, (i + 1) * size) for i in range(chunks)]
    mids = [spread(mid_low[span]) for span in spans]
    forward = [mlp_forward(mid, w_own, w_other) for mid in mids]
    grad_three = 0.0
    output_low, mlp_grads = [], []
    for span, (part, _, _) in zip(spans, forward):
        post_mlp, pull_mlp = jax.vjp(rms_gain, collect(part), gain_f[:, 3])
        output_low.append((residual_mid[span] + post_mlp).astype(BF))
        mlp_grad, gain_part_three = pull_mlp(out_grad[span])
        grad_three = grad_three + gain_part_three
        mlp_grads.append(spread(mlp_grad.astype(BF)))
    output_low = jnp.concatenate(output_low, axis=0)
    backward = [
        mlp_backward(grad, gate_up, w_own, w_other)
        for grad, (_, gate_up, _) in zip(mlp_grads, forward)
    ]
    mid_grad = jnp.concatenate([collect(part) for part, _ in backward], axis=0)

    def shard_sum(lefts, rights, cols):
        def product(low):
            total = 0.0
            for left, right in zip(lefts, rights):
                total = total + dot(left, right[:, low : low + cols], TN)
            return total

        other = product(cols).astype(BF)
        grad = (product(0) + flip(other, 1).astype(F32)).astype(BF)
        summed = lax.psum_scatter(grad, "ctx", scatter_dimension=0, tiled=True)
        back = lax.all_to_all(
            summed.reshape(dp_count, rows, cols), "dp", split_axis=0, concat_axis=0, tiled=True
        )
        return [
            back[:, :, low : low + units]
            .transpose(1, 0, 2)
            .reshape(rows, dp_count * units)[:, :FF]
            .astype(F32)
            for low in range(0, cols, units)
        ]

    (sum_down,) = shard_sum(mlp_grads, [hidden for _, _, hidden in forward], units)
    sum_gate, sum_up = shard_sum(mids, [grad for _, grad in backward], 2 * units)

    resid_part, grad_two = pull_mid(mid_grad)
    residual_grad = out_grad + resid_part
    attn_grad, grad_one = pull_attn(residual_grad)
    attn_low = attn_grad.astype(BF)
    grad_out = jnp.einsum("td,tc->dc", attn_low, mixed_low, preferred_element_type=F32)
    row_shape = (z_count, dp_count, rows)
    sum_out = scatter_rows(grad_out.astype(BF).reshape(row_shape + (Q_COLS,)))
    mixed_grad = jnp.dot(attn_low, w_out, preferred_element_type=F32).astype(BF)
    query_grads, key_value_part = attend_back(
        info, query_low, mixed_grad, mixed_low, inverse_total, key_value
    )
    key_value_grad = scatter_line(key_value_part.reshape(z_count, tok_rows, 2 * HD), "ctx")
    raw_query, raw_key, grad_head = pull_qk(
        (query_grads.reshape(tok_rows, H, HD), key_value_grad[:, :HD])
    )
    proj_low = jnp.concatenate([raw_query, raw_key, key_value_grad[:, HD:]], axis=1).astype(BF)
    grad_qkv = jnp.einsum("td,tc->dc", normed_low, proj_low, preferred_element_type=F32)
    in_part = jnp.einsum("tc,dc->td", proj_low, w_qkv, preferred_element_type=F32)
    input_part, grad_zero = pull_in(in_part)
    grad_input_low = (residual_grad + input_part).astype(BF)

    gain_grads = jnp.stack([grad_zero, grad_one, grad_two, grad_three], axis=1)
    gain_grads = gain_grads.reshape(row_shape + (4,))
    head_grads = grad_head.reshape(dp_count, z_count, head_rows, 2).transpose(1, 0, 2, 3)
    side = jnp.zeros(row_shape + (LANES,), BF)
    side = side.at[..., :4].set(gain_grads.astype(BF))
    side = side.at[..., :head_rows, 4:6].set(head_grads.astype(BF))
    qkv_parts = jnp.concatenate(
        [grad_qkv.astype(BF).reshape(row_shape + (START_GATE,)), side], axis=-1
    )
    sum_first = scatter_rows(qkv_parts)
    sum_qkv = sum_first[:, :START_GATE]
    sum_gains = sum_first[:, START_GATE : START_GATE + 4]
    sum_head = sum_first[:head_rows, START_GATE + 4 : START_GATE + 6]

    output = lax.dot_general(
        output_low, place, (((1,), (1,)), ((), ())), preferred_element_type=F32
    ).astype(BF)
    grad_input = lax.dot_general(
        grad_input_low, place, (((1,), (1,)), ((), ())), preferred_element_type=F32
    ).astype(BF)

    sum_weights = jnp.concatenate(
        [sum_qkv, sum_gate, sum_up, sum_out, sum_down], axis=1
    )
    new_w, first_w, second_w = adamw(
        weights, sum_weights, moment_weights, square_weights, RATE_WEIGHTS, WEIGHT_DECAY
    )
    new_g, first_g, second_g = adamw(
        norm_gains, sum_gains, moment_gains, square_gains, RATE_GAINS, 0.0
    )
    new_h, first_h, second_h = adamw(
        head_gains, sum_head, moment_head, square_head, RATE_GAINS, 0.0
    )
    return (
        output,
        grad_input,
        new_w,
        new_g,
        new_h,
        first_w,
        first_g,
        first_h,
        second_w,
        second_g,
        second_h,
        new_w.astype(BF),
    )


def solution(mesh):
    rows = P(("dp", "ctx"), None)
    in_specs = (rows, rows, P("dp")) + (rows,) * 9
    return jax.shard_map(
        body, mesh=mesh, in_specs=in_specs, out_specs=(rows,) * 12, check_vma=False
    )
```

```python
import numpy as np
import jax
import jax.numpy as jnp
from jax import lax
from jax.experimental import pallas as pl
from jax.experimental.pallas import tpu as pltpu
from jax.sharding import PartitionSpec as P

H = 4
HD = 256
FF = 6912
STEP = 10


NORM_EPS = 1e-06
ROPE_BASE = 1000000.0
QUERY_SCALE = 0.0625
BETA_ONE = 0.9
BETA_TWO = 0.95
ADAM_EPS = 1e-08
RATE_WEIGHTS = 0.03
RATE_GAINS = 0.1
WEIGHT_DECAY = 0.1
NEG_LARGE = -1e30

LANES = 128
Q_COLS = H * HD
START_GATE = Q_COLS + 2 * HD
START_OUT = START_GATE + 2 * FF
START_DOWN = START_OUT + Q_COLS
BF = jnp.bfloat16
F32 = jnp.float32


def block_positions(slots, rows, count):
    half_rows = rows // 2
    device = slots // rows
    within = slots % rows
    block = jnp.where(within < half_rows, device, 2 * count - 1 - device)
    return block * half_rows + within % half_rows


def rms_gain(values, gain):
    return values * lax.rsqrt(jnp.mean(values * values, axis=-1, keepdims=True) + NORM_EPS) * gain


def rotate(values, positions):
    half_dim = values.shape[-1] // 2
    freqs = jnp.power(ROPE_BASE, -2.0 * jnp.arange(half_dim).astype(jnp.float32) / values.shape[-1])
    angles = positions.astype(jnp.float32)[:, None] * freqs[None, :]
    cosine = jnp.cos(angles)[:, None, :]
    sine = jnp.sin(angles)[:, None, :]
    first = values[..., :half_dim]
    second = values[..., half_dim:]
    return jnp.concatenate(
        [first * cosine - second * sine, second * cosine + first * sine], axis=-1
    )


def adamw(weight, grad, first, second, rate, decay):
    first_new = BETA_ONE * first + (1.0 - BETA_ONE) * grad
    second_new = BETA_TWO * second + (1.0 - BETA_TWO) * grad * grad
    update = (
        first_new
        / (1.0 - BETA_ONE**STEP)
        / (jnp.sqrt(second_new / (1.0 - BETA_TWO**STEP)) + ADAM_EPS)
    )
    return (weight - rate * (update + decay * weight), first_new, second_new)


def shift(values, axis, distance):
    count = lax.axis_size(axis)
    return lax.ppermute(values, axis, [((i + distance) % count, i) for i in range(count)])


def flip(values, bit):
    return lax.ppermute(values, "dp", [(i ^ bit, i) for i in range(lax.axis_size("dp"))])


def my_bit(bit):
    return (lax.axis_index("dp") // bit) % 2


def chip_orders():
    bits = [1 << i for i in range(1, lax.axis_size("dp").bit_length() - 1)]
    return bits, bits[::-1]


def place_blocks(blocks, axis):
    count, me = len(blocks), lax.axis_index(axis)
    return jnp.stack([lax.select_n((j - me) % count, *blocks) for j in range(count)])


def gather_direct(values, axis):
    count = lax.axis_size(axis)
    blocks = [values] + [shift(values, axis, distance) for distance in range(1, count)]
    return place_blocks(blocks, axis)


def scatter_parts(parts, axis):
    count, me = lax.axis_size(axis), lax.axis_index(axis)
    return [
        lax.dynamic_index_in_dim(parts, (me - distance) % count, 0, keepdims=False)
        for distance in range(count)
    ]


def scatter_direct(slices, axis):
    total = slices[0].astype(F32)
    for distance, mine in enumerate(slices[1:], 1):
        total = total + shift(mine.astype(BF), axis, distance).astype(F32)
    return total


def side_by_side(own, other):
    mine = my_bit(1)
    return jnp.concatenate(
        [jnp.where(mine == 0, own, other), jnp.where(mine == 0, other, own)], axis=-1
    )


def halves_of(values):
    cols = values.shape[-1] // 2
    mine = my_bit(1)
    keep = lax.dynamic_slice_in_dim(values, mine * cols, cols, values.ndim - 1)
    send = lax.dynamic_slice_in_dim(values, (1 - mine) * cols, cols, values.ndim - 1)
    return keep, send


def column_spans(cols):
    half = cols // 2 // LANES * LANES
    return ((0, half), (half, cols))


def gather_rows(shard, after=None):
    rows, cols = shard.shape
    keep, send = halves_of(shard)
    got, mine = flip(send, 1), my_bit(1)
    pair = jnp.concatenate([jnp.where(mine == 0, keep, got), jnp.where(mine == 0, got, keep)])
    z_block = gather_direct(pair, "ctx")
    if after is not None:
        z_block = tie(z_block, after)
    parts = []
    for (low, high), bits in zip(column_spans(cols // 2), chip_orders()):
        part, done = z_block[..., low:high], []
        for bit in bits:
            got, mine = flip(part, bit), my_bit(bit)
            at = 1 + sum(other > bit for other in done)
            part = jnp.stack(
                [jnp.where(mine == 0, part, got), jnp.where(mine == 0, got, part)], axis=at
            )
            done.append(bit)
        parts.append(part.reshape(-1, high - low))
    own = jnp.concatenate(parts, axis=-1)
    return side_by_side(own, flip(own, 1))


def scatter_cols(parts, bits):
    return scatter_cols_sent(parts, bits)[0]


def scatter_cols_sent(parts, bits):
    part, first = parts.astype(BF), None
    for bit in bits:
        cols, mine = part.shape[1] // 2, my_bit(bit)
        keep = lax.dynamic_slice_in_dim(part, mine * cols, cols, 1)
        send = lax.dynamic_slice_in_dim(part, (1 - mine) * cols, cols, 1)
        first = send if first is None else first
        part = (keep.astype(F32) + flip(send, bit).astype(F32)).astype(BF)
    return part, first


def columns_back(blocks, bits):
    count, rows, cols = blocks.shape
    axes = sorted(bits, reverse=True)
    blocks = blocks.reshape((2,) * len(bits) + (rows, cols))
    order = [len(bits)] + [axes.index(bit) for bit in bits] + [len(bits) + 1]
    return blocks.transpose(order).reshape(rows, count * cols).astype(F32)


def spread_step(parts, step):
    return [(part, flip(part, bits[step])) for part, bits in zip(parts, chip_orders())]


def joined(pairs):
    return [jnp.concatenate(pair, axis=0) for pair in pairs]


def spread_start(values):
    half = values.shape[0] // 2
    parts = [values[:half], values[half:]]
    for step in range(len(chip_orders()[0]) - 1):
        parts = joined(spread_step(parts, step))
    return parts


def spread_end(parts):
    return joined(spread_step(parts, len(chip_orders()[0]) - 1))


def collect(parts, after=None):
    half = parts.shape[0] // 2
    parts = [parts[:half], parts[half:]]
    count = len(chip_orders()[0])
    sent = []
    for step in reversed(range(count)):
        sums, sends = [], []
        for part, bits in zip(parts, chip_orders()):
            size = part.shape[0] // 2
            send = part[size:].astype(BF)
            sends.append(tie(send, after) if after is not None and step == 0 else send)
            got = flip(sends[-1], bits[step])
            sums.append(part[:size].astype(F32) + got.astype(F32))
        parts = sums
        sent.append(sends)
    return jnp.concatenate(parts, axis=0), sent


def tie_all(value, others):
    for other in others:
        value = tie(value, other)
    return value


def pad_cols(values, cols):
    return jnp.pad(values, ((0, 0), (0, cols - values.shape[1])))


VMEM_LIMIT = 60 * 1024 * 1024
NO_COST = pl.CostEstimate(flops=0, bytes_accessed=0, transcendentals=0)
NT = (((1,), (1,)), ((), ()))
TN = (((0,), (0,)), ((), ()))


def dot(left, right, dims=(((1,), (0,)), ((), ()))):
    return lax.dot_general(left, right, dims, preferred_element_type=F32)


def whole(shape):
    return pl.BlockSpec(shape, lambda i: (0,) * len(shape))


def tie_kernel(value_ref, other_ref, out_ref):
    del value_ref, other_ref, out_ref


def tie(value, other):
    return pl.pallas_call(
        tie_kernel,
        out_shape=jax.ShapeDtypeStruct(value.shape, value.dtype),
        in_specs=[pl.BlockSpec(memory_space=pl.ANY)] * 2,
        out_specs=pl.BlockSpec(memory_space=pl.ANY),
        input_output_aliases={0: 0},
        compiler_params=pltpu.CompilerParams(has_side_effects=True),
        cost_estimate=NO_COST,
    )(value, other)


def key_row(block, rows, count):
    first = block * 2 * rows
    second = (2 * count - 1 - block) * 2 * rows + rows
    return pl.multiple_of(jnp.where(block < count, first, second), rows)


def key_bias(block, rows, length):
    spots = block * rows + lax.broadcasted_iota(jnp.int32, (1, rows), 1)
    return jnp.where(spots < length, 0.0, NEG_LARGE)


def attend_kernel(info_ref, query_ref, kv_ref, mixed_ref, total_ref, acc_ref, sum_ref):
    rows = query_ref.shape[0]
    count = kv_ref.shape[0] // (2 * rows)
    place, length = info_ref[0], info_ref[1]
    mine = jnp.where(pl.program_id(0) == 0, place, 2 * count - 1 - place)
    acc_ref[...] = jnp.zeros_like(acc_ref)
    sum_ref[...] = jnp.zeros_like(sum_ref)

    def step(block, causal):
        at = pl.ds(key_row(block, rows, count), rows)
        keys, values = kv_ref[at, :HD], kv_ref[at, HD:]
        bias = key_bias(block, rows, length)
        for head in range(H):
            cols = slice(head * HD, (head + 1) * HD)
            scores = dot(query_ref[:, cols], keys, NT) + bias
            weight = jnp.exp(scores)
            if causal:
                row = lax.broadcasted_iota(jnp.int32, (rows, rows), 0)
                col = lax.broadcasted_iota(jnp.int32, (rows, rows), 1)
                weight = jnp.where(col <= row, weight, 0.0)
            parts = weight[:, :LANES]
            for low in range(LANES, rows, LANES):
                parts = parts + weight[:, low : low + LANES]
            sum_ref[:, head * LANES : (head + 1) * LANES] += parts
            acc_ref[:, cols] += dot(weight.astype(BF), values)

    def loop(block, carry):
        step(block, False)
        return carry

    lax.fori_loop(0, mine, loop, 0)
    step(mine, True)
    for head in range(H):
        cols = slice(head * HD, (head + 1) * HD)
        total = jnp.sum(sum_ref[:, head * LANES : (head + 1) * LANES], axis=1, keepdims=True)
        inverse = 1.0 / total
        mixed_ref[:, cols] = (acc_ref[:, cols] * inverse).astype(BF)
        total_ref[:, head * LANES : (head + 1) * LANES] = jnp.broadcast_to(
            inverse, (rows, LANES)
        )


def attend(info, query, kv):
    half = query.shape[0] // 2
    spec = lambda cols: pl.BlockSpec((half, cols), lambda i, info: (i, 0))
    return pl.pallas_call(
        attend_kernel,
        grid_spec=pltpu.PrefetchScalarGridSpec(
            num_scalar_prefetch=1,
            grid=(2,),
            in_specs=[spec(Q_COLS), pl.BlockSpec(kv.shape, lambda i, info: (0, 0))],
            out_specs=[spec(Q_COLS), spec(H * LANES)],
            scratch_shapes=[pltpu.VMEM((half, Q_COLS), F32), pltpu.VMEM((half, H * LANES), F32)],
        ),
        out_shape=[
            jax.ShapeDtypeStruct((2 * half, Q_COLS), BF),
            jax.ShapeDtypeStruct((2 * half, H * LANES), F32),
        ],
        compiler_params=pltpu.CompilerParams(vmem_limit_bytes=VMEM_LIMIT),
        cost_estimate=NO_COST,
    )(info, query, kv)


def attend_back_kernel(
    info_ref, query_ref, grad_ref, mixed_ref, total_ref, kv_ref, dq_ref, dkv_ref, acc_ref, dq_acc
):
    rows = query_ref.shape[0]
    count = kv_ref.shape[0] // (2 * rows)
    place, length = info_ref[0], info_ref[1]
    step_id = pl.program_id(0)
    mine = jnp.where(step_id == 0, place, 2 * count - 1 - place)

    @pl.when(step_id == 0)
    def _():
        acc_ref[...] = jnp.zeros_like(acc_ref)

    dq_acc[...] = jnp.zeros_like(dq_acc)
    delta, inverse = [], []
    for head in range(H):
        cols = slice(head * HD, (head + 1) * HD)
        delta.append(
            jnp.sum(
                grad_ref[:, cols].astype(F32) * mixed_ref[:, cols].astype(F32),
                axis=1,
                keepdims=True,
            )
        )
        inverse.append(total_ref[:, head * LANES : head * LANES + 1])

    def step(block, causal):
        at = pl.ds(key_row(block, rows, count), rows)
        keys, values = kv_ref[at, :HD], kv_ref[at, HD:]
        bias = key_bias(block, rows, length)
        dk = jnp.zeros((rows, HD), F32)
        dv = jnp.zeros((rows, HD), F32)
        for head in range(H):
            cols = slice(head * HD, (head + 1) * HD)
            query, grad = query_ref[:, cols], grad_ref[:, cols]
            weight = jnp.exp(dot(query, keys, NT) + bias) * inverse[head]
            if causal:
                row = lax.broadcasted_iota(jnp.int32, (rows, rows), 0)
                col = lax.broadcasted_iota(jnp.int32, (rows, rows), 1)
                weight = jnp.where(col <= row, weight, 0.0)
            score = (weight * (dot(grad, values, NT) - delta[head])).astype(BF)
            dq_acc[:, cols] += dot(score, keys)
            dk = dk + dot(score, query, TN)
            dv = dv + dot(weight.astype(BF), grad, TN)
        acc_ref[at, :HD] += dk
        acc_ref[at, HD:] += dv

    def loop(block, carry):
        step(block, False)
        return carry

    lax.fori_loop(0, mine, loop, 0)
    step(mine, True)
    dq_ref[...] = dq_acc[...]

    @pl.when(step_id == pl.num_programs(0) - 1)
    def _():
        dkv_ref[...] = acc_ref[...].astype(BF)


def attend_back(info, query, grad, mixed, total, kv):
    half = query.shape[0] // 2
    spec = lambda cols: pl.BlockSpec((half, cols), lambda i, info: (i, 0))
    full = pl.BlockSpec(kv.shape, lambda i, info: (0, 0))
    return pl.pallas_call(
        attend_back_kernel,
        grid_spec=pltpu.PrefetchScalarGridSpec(
            num_scalar_prefetch=1,
            grid=(2,),
            in_specs=[spec(Q_COLS), spec(Q_COLS), spec(Q_COLS), spec(H * LANES), full],
            out_specs=[spec(Q_COLS), full],
            scratch_shapes=[pltpu.VMEM(kv.shape, F32), pltpu.VMEM((half, Q_COLS), F32)],
        ),
        out_shape=[
            jax.ShapeDtypeStruct((2 * half, Q_COLS), F32),
            jax.ShapeDtypeStruct(kv.shape, BF),
        ],
        compiler_params=pltpu.CompilerParams(vmem_limit_bytes=VMEM_LIMIT),
        cost_estimate=NO_COST,
    )(info, query, grad, mixed, total, kv)


GELU_A = 0.7978845608028654
GELU_B = 0.044715


def mlp_up_kernel(x_ref, own_ref, other_ref, gate_up_ref, hidden_ref):
    units = own_ref.shape[1] // 2
    for k, w_ref in enumerate((own_ref, other_ref)):
        both = dot(x_ref[...], w_ref[...])
        gate_up_ref[:, k * 2 * units : (k + 1) * 2 * units] = both.astype(BF)
        gate, up = both[:, :units], both[:, units:]
        inner = jnp.tanh(GELU_A * gate * (1.0 + GELU_B * gate * gate))
        hidden = (0.5 * gate * (1.0 + inner) * up).astype(BF)
        hidden_ref[:, k * units : (k + 1) * units] = hidden


def mlp_down_kernel(hidden_ref, own_ref, other_ref, part_ref):
    units = own_ref.shape[1]
    total = dot(hidden_ref[:, :units], own_ref[...], NT)
    part_ref[...] = (total + dot(hidden_ref[:, units:], other_ref[...], NT)).astype(BF)


def mlp_tile(rows):
    return min(rows, 512)


def mlp_up(x, own, other):
    rows, width = x.shape
    units = own.shape[1] // 2
    tile = mlp_tile(rows)
    spec = lambda cols: pl.BlockSpec((tile, cols), lambda i: (i, 0))
    return pl.pallas_call(
        mlp_up_kernel,
        grid=(rows // tile,),
        in_specs=[spec(width), whole(own.shape), whole(own.shape)],
        out_specs=[spec(4 * units), spec(2 * units)],
        out_shape=[
            jax.ShapeDtypeStruct((rows, 4 * units), BF),
            jax.ShapeDtypeStruct((rows, 2 * units), BF),
        ],
        compiler_params=pltpu.CompilerParams(vmem_limit_bytes=VMEM_LIMIT),
        cost_estimate=NO_COST,
    )(x, own, other)


def mlp_down(hidden, own, other):
    rows, (width, units) = hidden.shape[0], own.shape
    tile = mlp_tile(rows)
    spec = lambda cols: pl.BlockSpec((tile, cols), lambda i: (i, 0))
    return pl.pallas_call(
        mlp_down_kernel,
        grid=(rows // tile,),
        in_specs=[spec(2 * units), whole(own.shape), whole(own.shape)],
        out_specs=spec(width),
        out_shape=jax.ShapeDtypeStruct((rows, width), BF),
        compiler_params=pltpu.CompilerParams(vmem_limit_bytes=VMEM_LIMIT),
        cost_estimate=NO_COST,
    )(hidden, own, other)


def mlp_back_kernel(
    grad_ref,
    gate_up_ref,
    own_ref,
    other_ref,
    own_down_ref,
    other_down_ref,
    part_ref,
    gate_up_grad_ref,
):
    units = own_down_ref.shape[1]
    total = None
    for k, (w_ref, down_ref) in enumerate(((own_ref, own_down_ref), (other_ref, other_down_ref))):
        base = k * 2 * units
        hidden_grad = dot(grad_ref[...], down_ref[...])
        gate = gate_up_ref[:, base : base + units].astype(F32)
        up = gate_up_ref[:, base + units : base + 2 * units].astype(F32)
        square = gate * gate
        inner = jnp.tanh(GELU_A * gate * (1.0 + GELU_B * square))
        half = 0.5 * (1.0 + inner)
        slope = half + 0.5 * gate * (1.0 - inner * inner) * (
            GELU_A * (1.0 + 3.0 * GELU_B * square)
        )
        gate_grad = (hidden_grad * up * slope).astype(BF)
        up_grad = (hidden_grad * (gate * half)).astype(BF)
        gate_up_grad_ref[:, base : base + units] = gate_grad
        gate_up_grad_ref[:, base + units : base + 2 * units] = up_grad
        part = dot(gate_up_grad_ref[:, base : base + 2 * units], w_ref[...], NT)
        total = part if total is None else total + part
    part_ref[...] = total.astype(BF)


def mlp_backward(grad, gate_up, weights):
    rows, width = grad.shape
    units = weights[2].shape[1]
    tile = mlp_tile(rows)
    spec = lambda cols: pl.BlockSpec((tile, cols), lambda i: (i, 0))
    return pl.pallas_call(
        mlp_back_kernel,
        grid=(rows // tile,),
        in_specs=[spec(width), spec(4 * units)] + [whole(w.shape) for w in weights],
        out_specs=[spec(width), spec(4 * units)],
        out_shape=[
            jax.ShapeDtypeStruct((rows, width), BF),
            jax.ShapeDtypeStruct((rows, 4 * units), BF),
        ],
        compiler_params=pltpu.CompilerParams(vmem_limit_bytes=VMEM_LIMIT),
        cost_estimate=NO_COST,
    )(grad, gate_up, *weights)


def products(lefts, rights, units, kind):
    rows, width = lefts[0].shape
    kinds = rights[0].shape[1] // (2 * units)
    left = pl.BlockSpec((rows, width), lambda j: (0, 0))
    right = pl.BlockSpec((rows, units), lambda j: (0, kind + kinds * (1 - j)))
    out = pl.BlockSpec((width, units), lambda j: (0, 0))
    shape = jax.ShapeDtypeStruct((width, units), BF)

    def kernel(*refs):
        left_refs, right_refs, (other_ref, own_ref, turned_ref) = refs[:2], refs[2:4], refs[4:]

        @pl.when(pl.program_id(0) == 0)
        def _():
            for k in range(2):
                turned_ref[:, k * rows : (k + 1) * rows] = left_refs[k][...].T

        total = dot(turned_ref[:, :rows], right_refs[0][...])
        total = (total + dot(turned_ref[:, rows:], right_refs[1][...])).astype(BF)

        @pl.when(pl.program_id(0) == 0)
        def _():
            other_ref[...] = total

        @pl.when(pl.program_id(0) == 1)
        def _():
            own_ref[...] = total

    return pl.pallas_call(
        kernel,
        grid=(2,),
        in_specs=[left, left, right, right],
        out_specs=[out, out],
        out_shape=[shape, shape],
        scratch_shapes=[pltpu.VMEM((width, 2 * rows), BF)],
        compiler_params=pltpu.CompilerParams(vmem_limit_bytes=VMEM_LIMIT),
        cost_estimate=NO_COST,
    )(*lefts, *rights)


def body(
    layer_input,
    cotangent,
    lengths,
    weights,
    norm_gains,
    head_gains,
    moment_weights,
    moment_gains,
    moment_head,
    square_weights,
    square_gains,
    square_head,
):
    rows = weights.shape[0]
    head_rows = head_gains.shape[0]
    width = layer_input.shape[1]
    dp_count, z_count = lax.axis_size("dp"), lax.axis_size("ctx")
    units = -(-FF // (dp_count * LANES)) * LANES

    weights_low = weights.astype(BF)
    gain_cols = jnp.zeros((max(rows, head_rows), LANES), BF)
    gain_cols = gain_cols.at[:rows, :4].set(norm_gains.astype(BF))
    gain_cols = gain_cols.at[:head_rows, 4:6].set(head_gains.astype(BF))[:rows]
    first_shard = jnp.concatenate([weights_low[:, :START_GATE], pad_cols(gain_cols, 2 * LANES)], axis=1)
    mlp_shard = jnp.concatenate(
        [
            pad_cols(weights_low[:, start : start + FF], dp_count * units)
            .reshape(rows, dp_count, units)
            .transpose(1, 0, 2)
            for start in (START_GATE, START_GATE + FF, START_DOWN)
        ],
        axis=2,
    )
    mlp_block = lax.all_to_all(mlp_shard, "dp", split_axis=0, concat_axis=0, tiled=True)
    mlp_block = mlp_block.reshape(dp_count * rows, 3 * units)
    gate_up_block = mlp_block[:, : 2 * units]
    gate_up_own = lax.all_gather(gate_up_block, "ctx", axis=0, tiled=True)
    first_full = gather_rows(first_shard, gate_up_block)
    w_qkv = first_full[:, :START_GATE]
    gain_part = first_full[:, START_GATE : START_GATE + LANES].astype(F32)
    gain_f = 1.0 + gain_part[:, :4]
    head_f = gain_part.reshape(z_count, dp_count, rows, LANES)[:, :, :head_rows, 4:6]
    head_f = 1.0 + head_f.transpose(1, 0, 2, 3).reshape(HD, 2)

    order = np.arange(width).reshape(dp_count, z_count, rows).transpose(1, 0, 2).reshape(width)
    place = (jnp.arange(width)[:, None] == jnp.asarray(order)[None, :]).astype(BF)

    tok_rows = layer_input.shape[0]
    ctx_count = z_count
    local_slots = lax.axis_index("ctx") * tok_rows + jnp.arange(tok_rows, dtype=jnp.int32)
    positions = block_positions(local_slots, tok_rows, ctx_count)
    seq_length = lengths[0]
    row_valid = positions < seq_length
    inputs = jnp.dot(layer_input, place, preferred_element_type=F32)
    cot = jnp.dot(cotangent, place, preferred_element_type=F32)
    normed_in, pull_in = jax.vjp(rms_gain, inputs, gain_f[:, 0])
    normed_low = normed_in.astype(BF)
    key_value_raw = jnp.dot(normed_low, w_qkv[:, Q_COLS:], preferred_element_type=F32)
    query_raw = jnp.dot(normed_low, w_qkv[:, :Q_COLS], preferred_element_type=F32)

    def query_part(query_arg, head_arg):
        return (
            rotate(rms_gain(query_arg.reshape(tok_rows, H, HD), head_arg), positions) * QUERY_SCALE
        )

    def key_part(key_arg, head_arg):
        return rotate(rms_gain(key_arg[:, None, :], head_arg), positions)[:, 0]

    keys, pull_key = jax.vjp(key_part, key_value_raw[:, :HD], head_f[:, 1])
    key_value = jnp.concatenate([keys.astype(BF), key_value_raw[:, HD:].astype(BF)], axis=1)
    w_out = gather_rows(tie(weights_low[:, START_OUT:START_DOWN], first_full))
    queries, pull_query = jax.vjp(query_part, query_raw, head_f[:, 0])
    query_low = queries.astype(BF).reshape(tok_rows, Q_COLS)
    key_value = tie_all(key_value, [gate_up_own, w_out, query_low])
    key_value = lax.all_gather(key_value, "ctx", axis=0, tiled=True)
    down_own = lax.all_gather(
        tie(mlp_block[:, 2 * units :], key_value), "ctx", axis=0, tiled=True
    )
    gate_up_weights = (gate_up_own, flip(gate_up_own, 1))
    info = jnp.stack([lax.axis_index("ctx"), seq_length]).astype(jnp.int32)
    mixed_low, inverse_total = attend(info, query_low, key_value)
    attn_proj = jnp.einsum("tc,dc->td", mixed_low, w_out, preferred_element_type=F32)
    post_attn, pull_attn = jax.vjp(rms_gain, attn_proj, gain_f[:, 1])
    residual_mid = inputs + post_attn
    normed_mid, pull_mid = jax.vjp(rms_gain, residual_mid, gain_f[:, 2])

    mid_low = normed_mid.astype(BF)
    out_grad = cot * row_valid[:, None].astype(F32)
    chunks = 2
    size = tok_rows // chunks
    spans = [slice(i * size, (i + 1) * size) for i in range(chunks)]
    assert chunks == 2
    mids = [None, None]
    starts = [spread_start(mid_low[span]) for span in spans]
    mids[0] = jnp.concatenate(spread_end(starts[0]), axis=0)
    mids[0] = tie_all(mids[0], starts[1] + [down_own])
    second = spread_end(starts[1])
    first_up = mlp_up(mids[0], *gate_up_weights)
    mids[1] = tie(jnp.concatenate(second, axis=0), first_up[1])
    forward = [first_up, mlp_up(mids[1], *gate_up_weights)]
    gate_ups, hiddens = (list(kind) for kind in zip(*forward))
    down_own = tie(down_own, mids[1])
    mlp_weights = gate_up_weights + (down_own, flip(down_own, 1))
    hiddens[0] = tie(hiddens[0], gate_ups[1])
    parts = [mlp_down(hiddens[0], *mlp_weights[2:])]
    first, sent = collect(parts[0])
    hiddens[1] = tie_all(hiddens[1], sent[0])
    parts.append(mlp_down(hiddens[1], *mlp_weights[2:]))
    grad_three = 0.0
    output_low, starts = [], []
    for i, span in enumerate(spans):
        mlp_proj = collect(parts[1], starts[0][0])[0] if i else first
        post_mlp, pull_mlp = jax.vjp(rms_gain, mlp_proj, gain_f[:, 3])
        output_low.append((residual_mid[span] + post_mlp).astype(BF))
        mlp_grad, gain_part_three = pull_mlp(out_grad[span])
        grad_three = grad_three + gain_part_three
        starts.append(spread_start(mlp_grad.astype(BF)))
    output_low = jnp.concatenate(output_low, axis=0)
    mlp_grads = [jnp.concatenate(spread_end(starts[0]), axis=0)]
    starts[1] = [tie(part, mlp_grads[0]) for part in starts[1]]
    mlp_grads[0] = tie(tie(mlp_grads[0], starts[1][0]), starts[1][1])
    second = spread_end(starts[1])

    def both_cores(other, own):
        return (own.astype(F32) + flip(other, 1).astype(F32)).astype(BF)

    def shard_sum(grad):
        return lax.psum_scatter(grad, "ctx", scatter_dimension=0, tiled=True)

    def to_rows(summed):
        return lax.all_to_all(
            summed.reshape(dp_count, rows, summed.shape[1]), "dp", 0, 0, tiled=True
        )

    backward = [mlp_backward(mlp_grads[0], gate_ups[0], mlp_weights)]
    mlp_grads.append(jnp.concatenate(second, axis=0))
    first, sent = collect(backward[0][0])
    hiddens = [tie_all(hidden, sent[0]) for hidden in hiddens]
    down_other, down_mine = products(mlp_grads, hiddens, units, 0)
    down_grad = both_cores(down_other, tie_all(down_mine, sent[1]))
    summed_down = shard_sum(down_grad)
    backward.append(mlp_backward(mlp_grads[1], tie(gate_ups[1], down_mine), mlp_weights))
    second, sent = collect(backward[1][0])
    mid_grad = jnp.concatenate([first, second], axis=0)
    gate_up_grads = [tie_all(grad, sent[1]) for _, grad in backward]
    gate_other, gate_mine = products(mids, gate_up_grads, units, 0)
    gate_grad = both_cores(gate_other, gate_mine)
    summed_gate = shard_sum(gate_grad)
    output = lax.dot_general(
        tie(output_low, gate_mine), place, NT, preferred_element_type=F32
    ).astype(BF)

    mid_grad = tie_all(mid_grad, [gate_mine, summed_down, output])
    resid_part, grad_two = pull_mid(mid_grad)
    residual_grad = out_grad + resid_part
    attn_grad, grad_one = pull_attn(residual_grad)
    attn_low = attn_grad.astype(BF)
    mixed_grad = jnp.dot(attn_low, w_out, preferred_element_type=F32).astype(BF)
    query_grads, key_value_part = attend_back(
        info, query_low, mixed_grad, mixed_low, inverse_total, key_value
    )
    key_value_grad = lax.psum_scatter(
        tie(key_value_part, summed_gate), "ctx", scatter_dimension=0, tiled=True
    ).astype(F32)
    gate_up_grads = [tie(grad, query_grads) for grad in gate_up_grads]
    up_other, up_mine = products(mids, gate_up_grads, units, 1)
    up_grad = both_cores(up_other, up_mine)
    attn_late = tie(attn_low, query_grads)
    summed_up = shard_sum(tie(up_grad, key_value_grad))

    raw_query, grad_head_query = pull_query(query_grads.reshape(tok_rows, H, HD))
    query_grad_low = raw_query.astype(BF)
    bits_out, bits_query = ([1] + bits[::-1] for bits in chip_orders())
    out_share = scatter_cols(dot(attn_late, mixed_low, TN), bits_out)
    query_share = scatter_cols(dot(normed_low, query_grad_low, TN), bits_query)

    key_value_grad = tie(key_value_grad, up_grad)
    raw_key, grad_head_key = pull_key(key_value_grad[:, :HD])
    key_value_low = jnp.concatenate([raw_key, key_value_grad[:, HD:]], axis=1).astype(BF)
    late_bits, same_bits = bits_out[:2], bits_out[2:]
    late_share, sent = scatter_cols_sent(dot(normed_low, key_value_low, TN), late_bits)
    in_part = dot(query_grad_low, w_qkv[:, :Q_COLS], NT)
    in_part = in_part + dot(tie(key_value_low, sent), w_qkv[:, Q_COLS:], NT)
    input_part, grad_zero = pull_in(in_part)
    grad_input_low = (residual_grad + input_part).astype(BF)

    for bit in same_bits:
        late_share = (late_share.astype(F32) + flip(late_share, bit).astype(F32)).astype(BF)
    back = to_rows(jnp.concatenate([summed_gate, summed_up, summed_down], axis=1))
    early = shard_sum(jnp.concatenate([query_share, out_share], axis=1))
    late_share = tie(tie(late_share, back), early)
    slices = scatter_parts(late_share.reshape(z_count, -1, late_share.shape[1]), "ctx")
    back_attn = jnp.concatenate([early, scatter_direct(slices, "ctx").astype(BF)], axis=1)
    back_attn = to_rows(back_attn)
    share = Q_COLS // dp_count
    sum_query = columns_back(back_attn[:, :, :share], bits_query)
    sum_out = columns_back(back_attn[:, :, share : 2 * share], bits_out)
    back_late = back_attn[:, :, 2 * share :]
    back_late = back_late.reshape((2,) * len(bits_out) + back_late.shape[1:])
    for bit in sorted(same_bits):
        back_late = back_late[(slice(None),) * (len(bits_out) - bit.bit_length()) + (0,)]
    back_late = back_late.reshape((-1,) + back_late.shape[-2:])
    sum_late = columns_back(back_late, late_bits)

    gains = jnp.stack([grad_zero, grad_one, grad_two, grad_three]).reshape(-1)
    gains = jnp.concatenate([gains, grad_head_query, grad_head_key]).reshape(-1, LANES)
    for bit in bits_out:
        gains = gains + flip(gains, bit)
    gains = sum(shift(gains, "ctx", distance) for distance in range(1, z_count)) + gains
    gains = gains.reshape(-1)
    dp_me, z_me = lax.axis_index("dp"), lax.axis_index("ctx")
    sum_gains = lax.dynamic_slice_in_dim(
        gains[: 4 * width].reshape(4, width), (z_me * dp_count + dp_me) * rows, rows, 1
    ).T
    sum_head = lax.dynamic_slice_in_dim(
        gains[4 * width :].reshape(2, HD), (dp_me * z_count + z_me) * head_rows, head_rows, 1
    ).T
    sum_gate, sum_up, sum_down = (
        back[:, :, at : at + units]
        .transpose(1, 0, 2)
        .reshape(rows, dp_count * units)[:, :FF]
        .astype(F32)
        for at in (0, units, 2 * units)
    )

    grad_input = lax.dot_general(
        grad_input_low, place, (((1,), (1,)), ((), ())), preferred_element_type=F32
    ).astype(BF)

    sum_weights = jnp.concatenate(
        [sum_query, sum_late, sum_gate, sum_up, sum_out, sum_down], axis=1
    )
    new_w, first_w, second_w = adamw(
        weights, sum_weights, moment_weights, square_weights, RATE_WEIGHTS, WEIGHT_DECAY
    )
    new_g, first_g, second_g = adamw(
        norm_gains, sum_gains, moment_gains, square_gains, RATE_GAINS, 0.0
    )
    new_h, first_h, second_h = adamw(
        head_gains, sum_head, moment_head, square_head, RATE_GAINS, 0.0
    )
    return (
        output,
        grad_input,
        new_w,
        new_g,
        new_h,
        first_w,
        first_g,
        first_h,
        second_w,
        second_g,
        second_h,
        new_w.astype(BF),
    )


def solution(mesh):
    rows = P(("dp", "ctx"), None)
    in_specs = (rows, rows, P("dp")) + (rows,) * 9
    return jax.shard_map(
        body, mesh=mesh, in_specs=in_specs, out_specs=(rows,) * 12, check_vma=False
    )
```

```python
import numpy as np
import jax
import jax.numpy as jnp
from jax import lax
from jax.experimental import pallas as pl
from jax.experimental.pallas import tpu as pltpu
from jax.sharding import PartitionSpec as P

H = 4
HD = 256
FF = 6912
STEP = 10


NORM_EPS = 1e-06
ROPE_BASE = 1000000.0
QUERY_SCALE = 0.0625
BETA_ONE = 0.9
BETA_TWO = 0.95
ADAM_EPS = 1e-08
RATE_WEIGHTS = 0.03
RATE_GAINS = 0.1
WEIGHT_DECAY = 0.1
NEG_LARGE = -1e30

LANES = 128
Q_COLS = H * HD
START_GATE = Q_COLS + 2 * HD
START_OUT = START_GATE + 2 * FF
START_DOWN = START_OUT + Q_COLS
BF = jnp.bfloat16
F32 = jnp.float32


def block_positions(slots, rows, count):
    half_rows = rows // 2
    device = slots // rows
    within = slots % rows
    block = jnp.where(within < half_rows, device, 2 * count - 1 - device)
    return block * half_rows + within % half_rows


def rms_gain(values, gain):
    return values * lax.rsqrt(jnp.mean(values * values, axis=-1, keepdims=True) + NORM_EPS) * gain


def rotate(values, positions):
    half_dim = values.shape[-1] // 2
    freqs = jnp.power(ROPE_BASE, -2.0 * jnp.arange(half_dim).astype(jnp.float32) / values.shape[-1])
    angles = positions.astype(jnp.float32)[:, None] * freqs[None, :]
    cosine = jnp.cos(angles)[:, None, :]
    sine = jnp.sin(angles)[:, None, :]
    first = values[..., :half_dim]
    second = values[..., half_dim:]
    return jnp.concatenate(
        [first * cosine - second * sine, second * cosine + first * sine], axis=-1
    )


def adamw(weight, grad, first, second, rate, decay):
    first_new = BETA_ONE * first + (1.0 - BETA_ONE) * grad
    second_new = BETA_TWO * second + (1.0 - BETA_TWO) * grad * grad
    update = (
        first_new
        / (1.0 - BETA_ONE**STEP)
        / (jnp.sqrt(second_new / (1.0 - BETA_TWO**STEP)) + ADAM_EPS)
    )
    return (weight - rate * (update + decay * weight), first_new, second_new)


def shift(values, axis, distance):
    count = lax.axis_size(axis)
    return lax.ppermute(values, axis, [((i + distance) % count, i) for i in range(count)])


def flip(values, bit):
    return lax.ppermute(values, "dp", [(i ^ bit, i) for i in range(lax.axis_size("dp"))])


def my_bit(bit):
    return (lax.axis_index("dp") // bit) % 2


def chip_orders():
    bits = [1 << i for i in range(1, lax.axis_size("dp").bit_length() - 1)]
    return bits, bits[::-1]


def place_blocks(blocks, axis):
    count, me = len(blocks), lax.axis_index(axis)
    return jnp.stack([lax.select_n((j - me) % count, *blocks) for j in range(count)])


def gather_direct(values, axis):
    count = lax.axis_size(axis)
    blocks = [values] + [shift(values, axis, distance) for distance in range(1, count)]
    return place_blocks(blocks, axis)


def scatter_parts(parts, axis):
    count, me = lax.axis_size(axis), lax.axis_index(axis)
    return [
        lax.dynamic_index_in_dim(parts, (me - distance) % count, 0, keepdims=False)
        for distance in range(count)
    ]


def scatter_direct(slices, axis):
    total = slices[0].astype(F32)
    for distance, mine in enumerate(slices[1:], 1):
        total = total + shift(mine.astype(BF), axis, distance).astype(F32)
    return total


def side_by_side(own, other):
    mine = my_bit(1)
    return jnp.concatenate(
        [jnp.where(mine == 0, own, other), jnp.where(mine == 0, other, own)], axis=-1
    )


def halves_of(values):
    cols = values.shape[-1] // 2
    mine = my_bit(1)
    keep = lax.dynamic_slice_in_dim(values, mine * cols, cols, values.ndim - 1)
    send = lax.dynamic_slice_in_dim(values, (1 - mine) * cols, cols, values.ndim - 1)
    return keep, send


def column_spans(cols):
    half = cols // 2 // LANES * LANES
    return ((0, half), (half, cols))


def gather_rows(shard, after=None):
    rows, cols = shard.shape
    keep, send = halves_of(shard)
    got, mine = flip(send, 1), my_bit(1)
    pair = jnp.concatenate([jnp.where(mine == 0, keep, got), jnp.where(mine == 0, got, keep)])
    z_block = gather_direct(pair, "ctx")
    if after is not None:
        z_block = tie(z_block, after)
    parts = []
    for (low, high), bits in zip(column_spans(cols // 2), chip_orders()):
        part, done = z_block[..., low:high], []
        for bit in bits:
            got, mine = flip(part, bit), my_bit(bit)
            at = 1 + sum(other > bit for other in done)
            part = jnp.stack(
                [jnp.where(mine == 0, part, got), jnp.where(mine == 0, got, part)], axis=at
            )
            done.append(bit)
        parts.append(part.reshape(-1, high - low))
    own = jnp.concatenate(parts, axis=-1)
    return side_by_side(own, flip(own, 1))


def scatter_cols(parts, bits):
    return scatter_cols_sent(parts, bits)[0]


def scatter_cols_sent(parts, bits):
    part, first = parts.astype(BF), None
    for bit in bits:
        cols, mine = part.shape[1] // 2, my_bit(bit)
        keep = lax.dynamic_slice_in_dim(part, mine * cols, cols, 1)
        send = lax.dynamic_slice_in_dim(part, (1 - mine) * cols, cols, 1)
        first = send if first is None else first
        part = (keep.astype(F32) + flip(send, bit).astype(F32)).astype(BF)
    return part, first


def columns_back(blocks, bits):
    count, rows, cols = blocks.shape
    axes = sorted(bits, reverse=True)
    blocks = blocks.reshape((2,) * len(bits) + (rows, cols))
    order = [len(bits)] + [axes.index(bit) for bit in bits] + [len(bits) + 1]
    return blocks.transpose(order).reshape(rows, count * cols).astype(F32)


def spread_step(parts, step):
    return [(part, flip(part, bits[step])) for part, bits in zip(parts, chip_orders())]


def joined(pairs):
    return [jnp.concatenate(pair, axis=0) for pair in pairs]


def spread_start(values):
    half = values.shape[0] // 2
    parts = [values[:half], values[half:]]
    for step in range(len(chip_orders()[0]) - 1):
        parts = joined(spread_step(parts, step))
    return parts


def spread_end(parts):
    return joined(spread_step(parts, len(chip_orders()[0]) - 1))


def collect(parts, after=None):
    half = parts.shape[0] // 2
    parts = [parts[:half], parts[half:]]
    count = len(chip_orders()[0])
    sent = []
    for step in reversed(range(count)):
        sums, sends = [], []
        for part, bits in zip(parts, chip_orders()):
            size = part.shape[0] // 2
            send = part[size:].astype(BF)
            sends.append(tie(send, after) if after is not None and step == 0 else send)
            got = flip(sends[-1], bits[step])
            sums.append(part[:size].astype(F32) + got.astype(F32))
        parts = sums
        sent.append(sends)
    return jnp.concatenate(parts, axis=0), sent


def tie_all(value, others):
    for other in others:
        value = tie(value, other)
    return value


def pad_cols(values, cols):
    return jnp.pad(values, ((0, 0), (0, cols - values.shape[1])))


VMEM_LIMIT = 60 * 1024 * 1024
NO_COST = pl.CostEstimate(flops=0, bytes_accessed=0, transcendentals=0)
NT = (((1,), (1,)), ((), ()))
TN = (((0,), (0,)), ((), ()))


def dot(left, right, dims=(((1,), (0,)), ((), ()))):
    return lax.dot_general(left, right, dims, preferred_element_type=F32)


def whole(shape):
    return pl.BlockSpec(shape, lambda i: (0,) * len(shape))


def tie_kernel(value_ref, other_ref, out_ref):
    del value_ref, other_ref, out_ref


def tie(value, other):
    return pl.pallas_call(
        tie_kernel,
        out_shape=jax.ShapeDtypeStruct(value.shape, value.dtype),
        in_specs=[pl.BlockSpec(memory_space=pl.ANY)] * 2,
        out_specs=pl.BlockSpec(memory_space=pl.ANY),
        input_output_aliases={0: 0},
        compiler_params=pltpu.CompilerParams(has_side_effects=True),
        cost_estimate=NO_COST,
    )(value, other)


def key_row(block, rows, count):
    first = block * 2 * rows
    second = (2 * count - 1 - block) * 2 * rows + rows
    return pl.multiple_of(jnp.where(block < count, first, second), rows)


def key_bias(block, rows, length):
    spots = block * rows + lax.broadcasted_iota(jnp.int32, (1, rows), 1)
    return jnp.where(spots < length, 0.0, NEG_LARGE)


def attend_kernel(info_ref, query_ref, kv_ref, mixed_ref, total_ref, acc_ref, sum_ref):
    rows = query_ref.shape[0]
    count = kv_ref.shape[0] // (2 * rows)
    place, length = info_ref[0], info_ref[1]
    mine = jnp.where(pl.program_id(0) == 0, place, 2 * count - 1 - place)
    acc_ref[...] = jnp.zeros_like(acc_ref)
    sum_ref[...] = jnp.zeros_like(sum_ref)

    def step(block, causal):
        at = pl.ds(key_row(block, rows, count), rows)
        keys, values = kv_ref[at, :HD], kv_ref[at, HD:]
        bias = key_bias(block, rows, length)
        for head in range(H):
            cols = slice(head * HD, (head + 1) * HD)
            scores = dot(query_ref[:, cols], keys, NT) + bias
            weight = jnp.exp(scores)
            if causal:
                row = lax.broadcasted_iota(jnp.int32, (rows, rows), 0)
                col = lax.broadcasted_iota(jnp.int32, (rows, rows), 1)
                weight = jnp.where(col <= row, weight, 0.0)
            parts = weight[:, :LANES]
            for low in range(LANES, rows, LANES):
                parts = parts + weight[:, low : low + LANES]
            sum_ref[:, head * LANES : (head + 1) * LANES] += parts
            acc_ref[:, cols] += dot(weight.astype(BF), values)

    def loop(block, carry):
        step(block, False)
        return carry

    lax.fori_loop(0, mine, loop, 0)
    step(mine, True)
    for head in range(H):
        cols = slice(head * HD, (head + 1) * HD)
        total = jnp.sum(sum_ref[:, head * LANES : (head + 1) * LANES], axis=1, keepdims=True)
        inverse = 1.0 / total
        mixed_ref[:, cols] = (acc_ref[:, cols] * inverse).astype(BF)
        total_ref[:, head * LANES : (head + 1) * LANES] = jnp.broadcast_to(
            inverse, (rows, LANES)
        )


def attend(info, query, kv):
    half = query.shape[0] // 2
    spec = lambda cols: pl.BlockSpec((half, cols), lambda i, info: (i, 0))
    return pl.pallas_call(
        attend_kernel,
        grid_spec=pltpu.PrefetchScalarGridSpec(
            num_scalar_prefetch=1,
            grid=(2,),
            in_specs=[spec(Q_COLS), pl.BlockSpec(kv.shape, lambda i, info: (0, 0))],
            out_specs=[spec(Q_COLS), spec(H * LANES)],
            scratch_shapes=[pltpu.VMEM((half, Q_COLS), F32), pltpu.VMEM((half, H * LANES), F32)],
        ),
        out_shape=[
            jax.ShapeDtypeStruct((2 * half, Q_COLS), BF),
            jax.ShapeDtypeStruct((2 * half, H * LANES), F32),
        ],
        compiler_params=pltpu.CompilerParams(vmem_limit_bytes=VMEM_LIMIT),
        cost_estimate=NO_COST,
    )(info, query, kv)


def attend_back_kernel(
    info_ref, query_ref, grad_ref, mixed_ref, total_ref, kv_ref, dq_ref, dkv_ref, acc_ref, dq_acc
):
    rows = query_ref.shape[0]
    count = kv_ref.shape[0] // (2 * rows)
    place, length = info_ref[0], info_ref[1]
    step_id = pl.program_id(0)
    mine = jnp.where(step_id == 0, place, 2 * count - 1 - place)

    @pl.when(step_id == 0)
    def _():
        acc_ref[...] = jnp.zeros_like(acc_ref)

    dq_acc[...] = jnp.zeros_like(dq_acc)
    delta, inverse = [], []
    for head in range(H):
        cols = slice(head * HD, (head + 1) * HD)
        delta.append(
            jnp.sum(
                grad_ref[:, cols].astype(F32) * mixed_ref[:, cols].astype(F32),
                axis=1,
                keepdims=True,
            )
        )
        inverse.append(total_ref[:, head * LANES : head * LANES + 1])

    def step(block, causal):
        at = pl.ds(key_row(block, rows, count), rows)
        keys, values = kv_ref[at, :HD], kv_ref[at, HD:]
        bias = key_bias(block, rows, length)
        dk = jnp.zeros((rows, HD), F32)
        dv = jnp.zeros((rows, HD), F32)
        for head in range(H):
            cols = slice(head * HD, (head + 1) * HD)
            query, grad = query_ref[:, cols], grad_ref[:, cols]
            weight = jnp.exp(dot(query, keys, NT) + bias) * inverse[head]
            if causal:
                row = lax.broadcasted_iota(jnp.int32, (rows, rows), 0)
                col = lax.broadcasted_iota(jnp.int32, (rows, rows), 1)
                weight = jnp.where(col <= row, weight, 0.0)
            score = (weight * (dot(grad, values, NT) - delta[head])).astype(BF)
            dq_acc[:, cols] += dot(score, keys)
            dk = dk + dot(score, query, TN)
            dv = dv + dot(weight.astype(BF), grad, TN)
        acc_ref[at, :HD] += dk
        acc_ref[at, HD:] += dv

    def loop(block, carry):
        step(block, False)
        return carry

    lax.fori_loop(0, mine, loop, 0)
    step(mine, True)
    dq_ref[...] = dq_acc[...]

    @pl.when(step_id == pl.num_programs(0) - 1)
    def _():
        dkv_ref[...] = acc_ref[...].astype(BF)


def attend_back(info, query, grad, mixed, total, kv):
    half = query.shape[0] // 2
    spec = lambda cols: pl.BlockSpec((half, cols), lambda i, info: (i, 0))
    full = pl.BlockSpec(kv.shape, lambda i, info: (0, 0))
    return pl.pallas_call(
        attend_back_kernel,
        grid_spec=pltpu.PrefetchScalarGridSpec(
            num_scalar_prefetch=1,
            grid=(2,),
            in_specs=[spec(Q_COLS), spec(Q_COLS), spec(Q_COLS), spec(H * LANES), full],
            out_specs=[spec(Q_COLS), full],
            scratch_shapes=[pltpu.VMEM(kv.shape, F32), pltpu.VMEM((half, Q_COLS), F32)],
        ),
        out_shape=[
            jax.ShapeDtypeStruct((2 * half, Q_COLS), F32),
            jax.ShapeDtypeStruct(kv.shape, BF),
        ],
        compiler_params=pltpu.CompilerParams(vmem_limit_bytes=VMEM_LIMIT),
        cost_estimate=NO_COST,
    )(info, query, grad, mixed, total, kv)


GELU_A = 0.7978845608028654
GELU_B = 0.044715


def mlp_up_kernel(x_ref, own_ref, other_ref, gate_up_ref, hidden_ref):
    units = own_ref.shape[1] // 2
    for k, w_ref in enumerate((own_ref, other_ref)):
        both = dot(x_ref[...], w_ref[...])
        gate_up_ref[:, k * 2 * units : (k + 1) * 2 * units] = both.astype(BF)
        gate, up = both[:, :units], both[:, units:]
        inner = jnp.tanh(GELU_A * gate * (1.0 + GELU_B * gate * gate))
        hidden = (0.5 * gate * (1.0 + inner) * up).astype(BF)
        hidden_ref[:, k * units : (k + 1) * units] = hidden


def mlp_down_kernel(hidden_ref, own_ref, other_ref, part_ref):
    units = own_ref.shape[1]
    total = dot(hidden_ref[:, :units], own_ref[...], NT)
    part_ref[...] = (total + dot(hidden_ref[:, units:], other_ref[...], NT)).astype(BF)


def mlp_tile(rows):
    return min(rows, 512)


def mlp_up(x, own, other):
    rows, width = x.shape
    units = own.shape[1] // 2
    tile = mlp_tile(rows)
    spec = lambda cols: pl.BlockSpec((tile, cols), lambda i: (i, 0))
    return pl.pallas_call(
        mlp_up_kernel,
        grid=(rows // tile,),
        in_specs=[spec(width), whole(own.shape), whole(own.shape)],
        out_specs=[spec(4 * units), spec(2 * units)],
        out_shape=[
            jax.ShapeDtypeStruct((rows, 4 * units), BF),
            jax.ShapeDtypeStruct((rows, 2 * units), BF),
        ],
        compiler_params=pltpu.CompilerParams(vmem_limit_bytes=VMEM_LIMIT),
        cost_estimate=NO_COST,
    )(x, own, other)


def mlp_down(hidden, own, other):
    rows, (width, units) = hidden.shape[0], own.shape
    tile = mlp_tile(rows)
    spec = lambda cols: pl.BlockSpec((tile, cols), lambda i: (i, 0))
    return pl.pallas_call(
        mlp_down_kernel,
        grid=(rows // tile,),
        in_specs=[spec(2 * units), whole(own.shape), whole(own.shape)],
        out_specs=spec(width),
        out_shape=jax.ShapeDtypeStruct((rows, width), BF),
        compiler_params=pltpu.CompilerParams(vmem_limit_bytes=VMEM_LIMIT),
        cost_estimate=NO_COST,
    )(hidden, own, other)


def mlp_back_kernel(
    grad_ref,
    gate_up_ref,
    own_ref,
    other_ref,
    own_down_ref,
    other_down_ref,
    part_ref,
    gate_up_grad_ref,
):
    units = own_down_ref.shape[1]
    total = None
    for k, (w_ref, down_ref) in enumerate(((own_ref, own_down_ref), (other_ref, other_down_ref))):
        base = k * 2 * units
        hidden_grad = dot(grad_ref[...], down_ref[...])
        gate = gate_up_ref[:, base : base + units].astype(F32)
        up = gate_up_ref[:, base + units : base + 2 * units].astype(F32)
        square = gate * gate
        inner = jnp.tanh(GELU_A * gate * (1.0 + GELU_B * square))
        half = 0.5 * (1.0 + inner)
        slope = half + 0.5 * gate * (1.0 - inner * inner) * (
            GELU_A * (1.0 + 3.0 * GELU_B * square)
        )
        gate_grad = (hidden_grad * up * slope).astype(BF)
        up_grad = (hidden_grad * (gate * half)).astype(BF)
        gate_up_grad_ref[:, base : base + units] = gate_grad
        gate_up_grad_ref[:, base + units : base + 2 * units] = up_grad
        part = dot(gate_up_grad_ref[:, base : base + 2 * units], w_ref[...], NT)
        total = part if total is None else total + part
    part_ref[...] = total.astype(BF)


def mlp_backward(grad, gate_up, weights):
    rows, width = grad.shape
    units = weights[2].shape[1]
    tile = mlp_tile(rows)
    spec = lambda cols: pl.BlockSpec((tile, cols), lambda i: (i, 0))
    return pl.pallas_call(
        mlp_back_kernel,
        grid=(rows // tile,),
        in_specs=[spec(width), spec(4 * units)] + [whole(w.shape) for w in weights],
        out_specs=[spec(width), spec(4 * units)],
        out_shape=[
            jax.ShapeDtypeStruct((rows, width), BF),
            jax.ShapeDtypeStruct((rows, 4 * units), BF),
        ],
        compiler_params=pltpu.CompilerParams(vmem_limit_bytes=VMEM_LIMIT),
        cost_estimate=NO_COST,
    )(grad, gate_up, *weights)


def products(lefts, rights, units, kind):
    rows, width = lefts[0].shape
    kinds = rights[0].shape[1] // (2 * units)
    left = pl.BlockSpec((rows, width), lambda j: (0, 0))
    right = pl.BlockSpec((rows, units), lambda j: (0, kind + kinds * (1 - j)))
    out = pl.BlockSpec((width, units), lambda j: (0, 0))
    shape = jax.ShapeDtypeStruct((width, units), BF)

    def kernel(*refs):
        left_refs, right_refs, (other_ref, own_ref, turned_ref) = refs[:2], refs[2:4], refs[4:]

        @pl.when(pl.program_id(0) == 0)
        def _():
            for k in range(2):
                turned_ref[:, k * rows : (k + 1) * rows] = left_refs[k][...].T

        total = dot(turned_ref[:, :rows], right_refs[0][...])
        total = (total + dot(turned_ref[:, rows:], right_refs[1][...])).astype(BF)

        @pl.when(pl.program_id(0) == 0)
        def _():
            other_ref[...] = total

        @pl.when(pl.program_id(0) == 1)
        def _():
            own_ref[...] = total

    return pl.pallas_call(
        kernel,
        grid=(2,),
        in_specs=[left, left, right, right],
        out_specs=[out, out],
        out_shape=[shape, shape],
        scratch_shapes=[pltpu.VMEM((width, 2 * rows), BF)],
        compiler_params=pltpu.CompilerParams(vmem_limit_bytes=VMEM_LIMIT),
        cost_estimate=NO_COST,
    )(*lefts, *rights)


def body(
    layer_input,
    cotangent,
    lengths,
    weights,
    norm_gains,
    head_gains,
    moment_weights,
    moment_gains,
    moment_head,
    square_weights,
    square_gains,
    square_head,
):
    rows = weights.shape[0]
    head_rows = head_gains.shape[0]
    width = layer_input.shape[1]
    dp_count, z_count = lax.axis_size("dp"), lax.axis_size("ctx")
    units = -(-FF // (dp_count * LANES)) * LANES

    weights_low = weights.astype(BF)
    gain_cols = jnp.zeros((max(rows, head_rows), LANES), BF)
    gain_cols = gain_cols.at[:rows, :4].set(norm_gains.astype(BF))
    gain_cols = gain_cols.at[:head_rows, 4:6].set(head_gains.astype(BF))[:rows]
    first_shard = jnp.concatenate([weights_low[:, :START_GATE], pad_cols(gain_cols, 2 * LANES)], axis=1)
    mlp_shard = jnp.concatenate(
        [
            pad_cols(weights_low[:, start : start + FF], dp_count * units)
            .reshape(rows, dp_count, units)
            .transpose(1, 0, 2)
            for start in (START_GATE, START_GATE + FF, START_DOWN)
        ],
        axis=2,
    )
    mlp_block = lax.all_to_all(mlp_shard, "dp", split_axis=0, concat_axis=0, tiled=True)
    mlp_block = mlp_block.reshape(dp_count * rows, 3 * units)
    gate_up_block = mlp_block[:, : 2 * units]
    gate_up_own = lax.all_gather(gate_up_block, "ctx", axis=0, tiled=True)
    first_full = gather_rows(first_shard, gate_up_block)
    w_qkv = first_full[:, :START_GATE]
    gain_part = first_full[:, START_GATE : START_GATE + LANES].astype(F32)
    gain_f = 1.0 + gain_part[:, :4]
    head_f = gain_part.reshape(z_count, dp_count, rows, LANES)[:, :, :head_rows, 4:6]
    head_f = 1.0 + head_f.transpose(1, 0, 2, 3).reshape(HD, 2)

    order = np.arange(width).reshape(dp_count, z_count, rows).transpose(1, 0, 2).reshape(width)
    place = (jnp.arange(width)[:, None] == jnp.asarray(order)[None, :]).astype(BF)

    tok_rows = layer_input.shape[0]
    ctx_count = z_count
    local_slots = lax.axis_index("ctx") * tok_rows + jnp.arange(tok_rows, dtype=jnp.int32)
    positions = block_positions(local_slots, tok_rows, ctx_count)
    seq_length = lengths[0]
    row_valid = positions < seq_length
    inputs = jnp.dot(layer_input, place, preferred_element_type=F32)
    cot = jnp.dot(cotangent, place, preferred_element_type=F32)
    normed_in, pull_in = jax.vjp(rms_gain, inputs, gain_f[:, 0])
    normed_low = normed_in.astype(BF)
    key_value_raw = jnp.dot(normed_low, w_qkv[:, Q_COLS:], preferred_element_type=F32)
    query_raw = jnp.dot(normed_low, w_qkv[:, :Q_COLS], preferred_element_type=F32)

    def query_part(query_arg, head_arg):
        return (
            rotate(rms_gain(query_arg.reshape(tok_rows, H, HD), head_arg), positions) * QUERY_SCALE
        )

    def key_part(key_arg, head_arg):
        return rotate(rms_gain(key_arg[:, None, :], head_arg), positions)[:, 0]

    keys, pull_key = jax.vjp(key_part, key_value_raw[:, :HD], head_f[:, 1])
    key_value = jnp.concatenate([keys.astype(BF), key_value_raw[:, HD:].astype(BF)], axis=1)
    w_out = gather_rows(tie(weights_low[:, START_OUT:START_DOWN], first_full))
    queries, pull_query = jax.vjp(query_part, query_raw, head_f[:, 0])
    query_low = queries.astype(BF).reshape(tok_rows, Q_COLS)
    key_value = tie_all(key_value, [gate_up_own, w_out, query_low])
    key_value = lax.all_gather(key_value, "ctx", axis=0, tiled=True)
    down_own = lax.all_gather(
        tie(mlp_block[:, 2 * units :], key_value), "ctx", axis=0, tiled=True
    )
    gate_up_weights = (gate_up_own, flip(gate_up_own, 1))
    info = jnp.stack([lax.axis_index("ctx"), seq_length]).astype(jnp.int32)
    mixed_low, inverse_total = attend(info, query_low, key_value)
    attn_proj = jnp.einsum("tc,dc->td", mixed_low, w_out, preferred_element_type=F32)
    post_attn, pull_attn = jax.vjp(rms_gain, attn_proj, gain_f[:, 1])
    residual_mid = inputs + post_attn
    normed_mid, pull_mid = jax.vjp(rms_gain, residual_mid, gain_f[:, 2])

    mid_low = normed_mid.astype(BF)
    out_grad = cot * row_valid[:, None].astype(F32)
    chunks = 2
    size = tok_rows // chunks
    spans = [slice(i * size, (i + 1) * size) for i in range(chunks)]
    assert chunks == 2
    mids = [None, None]
    starts = [spread_start(mid_low[span]) for span in spans]
    mids[0] = jnp.concatenate(spread_end(starts[0]), axis=0)
    mids[0] = tie_all(mids[0], starts[1] + [down_own])
    second = spread_end(starts[1])
    first_up = mlp_up(mids[0], *gate_up_weights)
    mids[1] = tie(jnp.concatenate(second, axis=0), first_up[1])
    forward = [first_up, mlp_up(mids[1], *gate_up_weights)]
    gate_ups, hiddens = (list(kind) for kind in zip(*forward))
    down_own = tie(down_own, mids[1])
    mlp_weights = gate_up_weights + (down_own, flip(down_own, 1))
    hiddens[0] = tie(hiddens[0], gate_ups[1])
    parts = [mlp_down(hiddens[0], *mlp_weights[2:])]
    first, sent = collect(parts[0])
    hiddens[1] = tie_all(hiddens[1], sent[0])
    parts.append(mlp_down(hiddens[1], *mlp_weights[2:]))
    grad_three = 0.0
    output_low, starts = [], []
    for i, span in enumerate(spans):
        mlp_proj = collect(parts[1], starts[0][0])[0] if i else first
        post_mlp, pull_mlp = jax.vjp(rms_gain, mlp_proj, gain_f[:, 3])
        output_low.append((residual_mid[span] + post_mlp).astype(BF))
        mlp_grad, gain_part_three = pull_mlp(out_grad[span])
        grad_three = grad_three + gain_part_three
        starts.append(spread_start(mlp_grad.astype(BF)))
    output_low = jnp.concatenate(output_low, axis=0)
    mlp_grads = [jnp.concatenate(spread_end(starts[0]), axis=0)]
    starts[1] = [tie(part, mlp_grads[0]) for part in starts[1]]
    mlp_grads[0] = tie(tie(mlp_grads[0], starts[1][0]), starts[1][1])
    second = spread_end(starts[1])

    def both_cores(other, own):
        return (own.astype(F32) + flip(other, 1).astype(F32)).astype(BF)

    def shard_sum(grad):
        return lax.psum_scatter(grad, "ctx", scatter_dimension=0, tiled=True)

    def to_rows(summed):
        return lax.all_to_all(
            summed.reshape(dp_count, rows, summed.shape[1]), "dp", 0, 0, tiled=True
        )

    backward = [mlp_backward(mlp_grads[0], gate_ups[0], mlp_weights)]
    mlp_grads.append(jnp.concatenate(second, axis=0))
    first, sent = collect(backward[0][0])
    hiddens = [tie_all(hidden, sent[0]) for hidden in hiddens]
    down_other, down_mine = products(mlp_grads, hiddens, units, 0)
    down_grad = both_cores(down_other, tie_all(down_mine, sent[1]))
    summed_down = shard_sum(down_grad)
    backward.append(mlp_backward(mlp_grads[1], tie(gate_ups[1], down_mine), mlp_weights))
    second, sent = collect(backward[1][0])
    mid_grad = jnp.concatenate([first, second], axis=0)
    gate_up_grads = [tie_all(grad, sent[1]) for _, grad in backward]
    gate_other, gate_mine = products(mids, gate_up_grads, units, 0)
    gate_grad = both_cores(gate_other, gate_mine)
    summed_gate = shard_sum(gate_grad)
    output = lax.dot_general(
        tie(output_low, gate_mine), place, NT, preferred_element_type=F32
    ).astype(BF)

    mid_grad = tie_all(mid_grad, [gate_mine, summed_down, output])
    resid_part, grad_two = pull_mid(mid_grad)
    residual_grad = out_grad + resid_part
    attn_grad, grad_one = pull_attn(residual_grad)
    attn_low = attn_grad.astype(BF)
    mixed_grad = jnp.dot(attn_low, w_out, preferred_element_type=F32).astype(BF)
    query_grads, key_value_part = attend_back(
        info, query_low, mixed_grad, mixed_low, inverse_total, key_value
    )
    key_value_grad = lax.psum_scatter(
        tie(key_value_part, summed_gate), "ctx", scatter_dimension=0, tiled=True
    ).astype(F32)
    gate_up_grads = [tie(grad, query_grads) for grad in gate_up_grads]
    up_other, up_mine = products(mids, gate_up_grads, units, 1)
    up_grad = both_cores(up_other, up_mine)
    attn_late = tie(attn_low, query_grads)
    summed_up = shard_sum(tie(up_grad, key_value_grad))

    raw_query, grad_head_query = pull_query(query_grads.reshape(tok_rows, H, HD))
    query_grad_low = raw_query.astype(BF)
    bits_out, bits_query = ([1] + bits[::-1] for bits in chip_orders())
    out_share = scatter_cols(dot(attn_late, mixed_low, TN), bits_out)
    query_share = scatter_cols(dot(normed_low, query_grad_low, TN), bits_query)

    key_value_grad = tie(key_value_grad, up_grad)
    raw_key, grad_head_key = pull_key(key_value_grad[:, :HD])
    key_value_low = jnp.concatenate([raw_key, key_value_grad[:, HD:]], axis=1).astype(BF)
    late_bits, same_bits = bits_out[:2], bits_out[2:]
    late_share, sent = scatter_cols_sent(dot(normed_low, key_value_low, TN), late_bits[:1])
    in_part = dot(query_grad_low, w_qkv[:, :Q_COLS], NT)
    in_part = in_part + dot(tie(key_value_low, sent), w_qkv[:, Q_COLS:], NT)
    input_part, grad_zero = pull_in(in_part)
    grad_input_low = (residual_grad + input_part).astype(BF)

    back = to_rows(jnp.concatenate([summed_gate, summed_up, summed_down], axis=1))
    early = shard_sum(jnp.concatenate([query_share, out_share], axis=1))
    slices = scatter_parts(late_share.reshape(z_count, -1, late_share.shape[1]), "ctx")
    late_rows = tie(tie(scatter_direct(slices, "ctx").astype(BF), back), early)
    late_rows = scatter_cols(late_rows, late_bits[1:])
    for bit in same_bits:
        late_rows = (late_rows.astype(F32) + flip(late_rows, bit).astype(F32)).astype(BF)
    back_attn = jnp.concatenate([early, late_rows], axis=1)
    back_attn = to_rows(back_attn)
    share = Q_COLS // dp_count
    sum_query = columns_back(back_attn[:, :, :share], bits_query)
    sum_out = columns_back(back_attn[:, :, share : 2 * share], bits_out)
    back_late = back_attn[:, :, 2 * share :]
    back_late = back_late.reshape((2,) * len(bits_out) + back_late.shape[1:])
    for bit in sorted(same_bits):
        back_late = back_late[(slice(None),) * (len(bits_out) - bit.bit_length()) + (0,)]
    back_late = back_late.reshape((-1,) + back_late.shape[-2:])
    sum_late = columns_back(back_late, late_bits)

    gains = jnp.stack([grad_zero, grad_one, grad_two, grad_three]).reshape(-1)
    gains = jnp.concatenate([gains, grad_head_query, grad_head_key]).reshape(-1, LANES)
    for bit in bits_out:
        gains = gains + flip(gains, bit)
    gains = sum(shift(gains, "ctx", distance) for distance in range(1, z_count)) + gains
    gains = gains.reshape(-1)
    dp_me, z_me = lax.axis_index("dp"), lax.axis_index("ctx")
    sum_gains = lax.dynamic_slice_in_dim(
        gains[: 4 * width].reshape(4, width), (z_me * dp_count + dp_me) * rows, rows, 1
    ).T
    sum_head = lax.dynamic_slice_in_dim(
        gains[4 * width :].reshape(2, HD), (dp_me * z_count + z_me) * head_rows, head_rows, 1
    ).T
    sum_gate, sum_up, sum_down = (
        back[:, :, at : at + units]
        .transpose(1, 0, 2)
        .reshape(rows, dp_count * units)[:, :FF]
        .astype(F32)
        for at in (0, units, 2 * units)
    )

    grad_input = lax.dot_general(
        grad_input_low, place, (((1,), (1,)), ((), ())), preferred_element_type=F32
    ).astype(BF)

    sum_weights = jnp.concatenate(
        [sum_query, sum_late, sum_gate, sum_up, sum_out, sum_down], axis=1
    )
    new_w, first_w, second_w = adamw(
        weights, sum_weights, moment_weights, square_weights, RATE_WEIGHTS, WEIGHT_DECAY
    )
    new_g, first_g, second_g = adamw(
        norm_gains, sum_gains, moment_gains, square_gains, RATE_GAINS, 0.0
    )
    new_h, first_h, second_h = adamw(
        head_gains, sum_head, moment_head, square_head, RATE_GAINS, 0.0
    )
    return (
        output,
        grad_input,
        new_w,
        new_g,
        new_h,
        first_w,
        first_g,
        first_h,
        second_w,
        second_g,
        second_h,
        new_w.astype(BF),
    )


def solution(mesh):
    rows = P(("dp", "ctx"), None)
    in_specs = (rows, rows, P("dp")) + (rows,) * 9
    return jax.shard_map(
        body, mesh=mesh, in_specs=in_specs, out_specs=(rows,) * 12, check_vma=False
    )
```

```python
import numpy as np
import jax
import jax.numpy as jnp
from jax import lax
from jax.experimental import pallas as pl
from jax.experimental.pallas import tpu as pltpu
from jax.sharding import PartitionSpec as P

H = 4
HD = 256
FF = 6912
STEP = 10


NORM_EPS = 1e-06
ROPE_BASE = 1000000.0
QUERY_SCALE = 0.0625
BETA_ONE = 0.9
BETA_TWO = 0.95
ADAM_EPS = 1e-08
RATE_WEIGHTS = 0.03
RATE_GAINS = 0.1
WEIGHT_DECAY = 0.1
NEG_LARGE = -1e30

LANES = 128
Q_COLS = H * HD
START_GATE = Q_COLS + 2 * HD
START_OUT = START_GATE + 2 * FF
START_DOWN = START_OUT + Q_COLS
BF = jnp.bfloat16
F32 = jnp.float32


def block_positions(slots, rows, count):
    half_rows = rows // 2
    device = slots // rows
    within = slots % rows
    block = jnp.where(within < half_rows, device, 2 * count - 1 - device)
    return block * half_rows + within % half_rows


def rms_gain(values, gain):
    return values * lax.rsqrt(jnp.mean(values * values, axis=-1, keepdims=True) + NORM_EPS) * gain


def rotate(values, positions):
    half_dim = values.shape[-1] // 2
    freqs = jnp.power(ROPE_BASE, -2.0 * jnp.arange(half_dim).astype(jnp.float32) / values.shape[-1])
    angles = positions.astype(jnp.float32)[:, None] * freqs[None, :]
    cosine = jnp.cos(angles)[:, None, :]
    sine = jnp.sin(angles)[:, None, :]
    first = values[..., :half_dim]
    second = values[..., half_dim:]
    return jnp.concatenate(
        [first * cosine - second * sine, second * cosine + first * sine], axis=-1
    )


def adamw(weight, grad, first, second, rate, decay):
    first_new = BETA_ONE * first + (1.0 - BETA_ONE) * grad
    second_new = BETA_TWO * second + (1.0 - BETA_TWO) * grad * grad
    update = (
        first_new
        / (1.0 - BETA_ONE**STEP)
        / (jnp.sqrt(second_new / (1.0 - BETA_TWO**STEP)) + ADAM_EPS)
    )
    return (weight - rate * (update + decay * weight), first_new, second_new)


def shift(values, axis, distance):
    count = lax.axis_size(axis)
    return lax.ppermute(values, axis, [((i + distance) % count, i) for i in range(count)])


def flip(values, bit):
    return lax.ppermute(values, "dp", [(i ^ bit, i) for i in range(lax.axis_size("dp"))])


def my_bit(bit):
    return (lax.axis_index("dp") // bit) % 2


def chip_orders():
    bits = [1 << i for i in range(1, lax.axis_size("dp").bit_length() - 1)]
    return bits, bits[::-1]


def place_blocks(blocks, axis):
    count, me = len(blocks), lax.axis_index(axis)
    return jnp.stack([lax.select_n((j - me) % count, *blocks) for j in range(count)])


def gather_direct(values, axis):
    count = lax.axis_size(axis)
    blocks = [values] + [shift(values, axis, distance) for distance in range(1, count)]
    return place_blocks(blocks, axis)


def scatter_parts(parts, axis):
    count, me = lax.axis_size(axis), lax.axis_index(axis)
    return [
        lax.dynamic_index_in_dim(parts, (me - distance) % count, 0, keepdims=False)
        for distance in range(count)
    ]


def scatter_direct(slices, axis):
    total = slices[0].astype(F32)
    for distance, mine in enumerate(slices[1:], 1):
        total = total + shift(mine.astype(BF), axis, distance).astype(F32)
    return total


def side_by_side(own, other):
    mine = my_bit(1)
    return jnp.concatenate(
        [jnp.where(mine == 0, own, other), jnp.where(mine == 0, other, own)], axis=-1
    )


def halves_of(values):
    cols = values.shape[-1] // 2
    mine = my_bit(1)
    keep = lax.dynamic_slice_in_dim(values, mine * cols, cols, values.ndim - 1)
    send = lax.dynamic_slice_in_dim(values, (1 - mine) * cols, cols, values.ndim - 1)
    return keep, send


def column_spans(cols):
    half = cols // 2 // LANES * LANES
    return ((0, half), (half, cols))


def gather_rows(shard, after=None):
    rows, cols = shard.shape
    keep, send = halves_of(shard)
    got, mine = flip(send, 1), my_bit(1)
    pair = jnp.concatenate([jnp.where(mine == 0, keep, got), jnp.where(mine == 0, got, keep)])
    z_block = gather_direct(pair, "ctx")
    if after is not None:
        z_block = tie(z_block, after)
    parts = []
    for (low, high), bits in zip(column_spans(cols // 2), chip_orders()):
        part, done = z_block[..., low:high], []
        for bit in bits:
            got, mine = flip(part, bit), my_bit(bit)
            at = 1 + sum(other > bit for other in done)
            part = jnp.stack(
                [jnp.where(mine == 0, part, got), jnp.where(mine == 0, got, part)], axis=at
            )
            done.append(bit)
        parts.append(part.reshape(-1, high - low))
    own = jnp.concatenate(parts, axis=-1)
    return side_by_side(own, flip(own, 1))


def scatter_cols(parts, bits):
    return scatter_cols_sent(parts, bits)[0]


def scatter_cols_sent(parts, bits):
    part, first = parts.astype(BF), None
    for bit in bits:
        cols, mine = part.shape[1] // 2, my_bit(bit)
        keep = lax.dynamic_slice_in_dim(part, mine * cols, cols, 1)
        send = lax.dynamic_slice_in_dim(part, (1 - mine) * cols, cols, 1)
        first = send if first is None else first
        part = (keep.astype(F32) + flip(send, bit).astype(F32)).astype(BF)
    return part, first


def columns_back(blocks, bits):
    count, rows, cols = blocks.shape
    axes = sorted(bits, reverse=True)
    blocks = blocks.reshape((2,) * len(bits) + (rows, cols))
    order = [len(bits)] + [axes.index(bit) for bit in bits] + [len(bits) + 1]
    return blocks.transpose(order).reshape(rows, count * cols).astype(F32)


def spread_step(parts, step):
    return [(part, flip(part, bits[step])) for part, bits in zip(parts, chip_orders())]


def joined(pairs):
    return [jnp.concatenate(pair, axis=0) for pair in pairs]


def spread_start(values):
    half = values.shape[0] // 2
    parts = [values[:half], values[half:]]
    for step in range(len(chip_orders()[0]) - 1):
        parts = joined(spread_step(parts, step))
    return parts


def spread_end(parts):
    return joined(spread_step(parts, len(chip_orders()[0]) - 1))


def collect(parts, after=None):
    half = parts.shape[0] // 2
    parts = [parts[:half], parts[half:]]
    count = len(chip_orders()[0])
    sent = []
    for step in reversed(range(count)):
        sums, sends = [], []
        for part, bits in zip(parts, chip_orders()):
            size = part.shape[0] // 2
            send = part[size:].astype(BF)
            sends.append(tie(send, after) if after is not None and step == 0 else send)
            got = flip(sends[-1], bits[step])
            sums.append(part[:size].astype(F32) + got.astype(F32))
        parts = sums
        sent.append(sends)
    return jnp.concatenate(parts, axis=0), sent


def tie_all(value, others):
    for other in others:
        value = tie(value, other)
    return value


def pad_cols(values, cols):
    return jnp.pad(values, ((0, 0), (0, cols - values.shape[1])))


VMEM_LIMIT = 60 * 1024 * 1024
NO_COST = pl.CostEstimate(flops=0, bytes_accessed=0, transcendentals=0)
NT = (((1,), (1,)), ((), ()))
TN = (((0,), (0,)), ((), ()))


def dot(left, right, dims=(((1,), (0,)), ((), ()))):
    return lax.dot_general(left, right, dims, preferred_element_type=F32)


def whole(shape):
    return pl.BlockSpec(shape, lambda i: (0,) * len(shape))


def tie_kernel(value_ref, other_ref, out_ref):
    del value_ref, other_ref, out_ref


def tie(value, other):
    return pl.pallas_call(
        tie_kernel,
        out_shape=jax.ShapeDtypeStruct(value.shape, value.dtype),
        in_specs=[pl.BlockSpec(memory_space=pl.ANY)] * 2,
        out_specs=pl.BlockSpec(memory_space=pl.ANY),
        input_output_aliases={0: 0},
        compiler_params=pltpu.CompilerParams(has_side_effects=True),
        cost_estimate=NO_COST,
    )(value, other)


def key_row(block, rows, count):
    first = block * 2 * rows
    second = (2 * count - 1 - block) * 2 * rows + rows
    return pl.multiple_of(jnp.where(block < count, first, second), rows)


def key_bias(block, rows, length):
    spots = block * rows + lax.broadcasted_iota(jnp.int32, (1, rows), 1)
    return jnp.where(spots < length, 0.0, NEG_LARGE)


def attend_kernel(info_ref, query_ref, kv_ref, mixed_ref, total_ref, acc_ref, sum_ref):
    rows = query_ref.shape[0]
    count = kv_ref.shape[0] // (2 * rows)
    place, length = info_ref[0], info_ref[1]
    mine = jnp.where(pl.program_id(0) == 0, place, 2 * count - 1 - place)
    acc_ref[...] = jnp.zeros_like(acc_ref)
    sum_ref[...] = jnp.zeros_like(sum_ref)

    def step(block, causal):
        at = pl.ds(key_row(block, rows, count), rows)
        keys, values = kv_ref[at, :HD], kv_ref[at, HD:]
        bias = key_bias(block, rows, length)
        for head in range(H):
            cols = slice(head * HD, (head + 1) * HD)
            scores = dot(query_ref[:, cols], keys, NT) + bias
            weight = jnp.exp(scores)
            if causal:
                row = lax.broadcasted_iota(jnp.int32, (rows, rows), 0)
                col = lax.broadcasted_iota(jnp.int32, (rows, rows), 1)
                weight = jnp.where(col <= row, weight, 0.0)
            parts = weight[:, :LANES]
            for low in range(LANES, rows, LANES):
                parts = parts + weight[:, low : low + LANES]
            sum_ref[:, head * LANES : (head + 1) * LANES] += parts
            acc_ref[:, cols] += dot(weight.astype(BF), values)

    def loop(block, carry):
        step(block, False)
        return carry

    lax.fori_loop(0, mine, loop, 0)
    step(mine, True)
    for head in range(H):
        cols = slice(head * HD, (head + 1) * HD)
        total = jnp.sum(sum_ref[:, head * LANES : (head + 1) * LANES], axis=1, keepdims=True)
        inverse = 1.0 / total
        mixed_ref[:, cols] = (acc_ref[:, cols] * inverse).astype(BF)
        total_ref[:, head * LANES : (head + 1) * LANES] = jnp.broadcast_to(
            inverse, (rows, LANES)
        )


def attend(info, query, kv):
    half = query.shape[0] // 2
    spec = lambda cols: pl.BlockSpec((half, cols), lambda i, info: (i, 0))
    return pl.pallas_call(
        attend_kernel,
        grid_spec=pltpu.PrefetchScalarGridSpec(
            num_scalar_prefetch=1,
            grid=(2,),
            in_specs=[spec(Q_COLS), pl.BlockSpec(kv.shape, lambda i, info: (0, 0))],
            out_specs=[spec(Q_COLS), spec(H * LANES)],
            scratch_shapes=[pltpu.VMEM((half, Q_COLS), F32), pltpu.VMEM((half, H * LANES), F32)],
        ),
        out_shape=[
            jax.ShapeDtypeStruct((2 * half, Q_COLS), BF),
            jax.ShapeDtypeStruct((2 * half, H * LANES), F32),
        ],
        compiler_params=pltpu.CompilerParams(vmem_limit_bytes=VMEM_LIMIT),
        cost_estimate=NO_COST,
    )(info, query, kv)


def attend_back_kernel(
    info_ref, query_ref, grad_ref, mixed_ref, total_ref, kv_ref, dq_ref, dkv_ref, acc_ref, dq_acc
):
    rows = query_ref.shape[0]
    count = kv_ref.shape[0] // (2 * rows)
    place, length = info_ref[0], info_ref[1]
    step_id = pl.program_id(0)
    mine = jnp.where(step_id == 0, place, 2 * count - 1 - place)

    @pl.when(step_id == 0)
    def _():
        acc_ref[...] = jnp.zeros_like(acc_ref)

    dq_acc[...] = jnp.zeros_like(dq_acc)
    delta, inverse = [], []
    for head in range(H):
        cols = slice(head * HD, (head + 1) * HD)
        delta.append(
            jnp.sum(
                grad_ref[:, cols].astype(F32) * mixed_ref[:, cols].astype(F32),
                axis=1,
                keepdims=True,
            )
        )
        inverse.append(total_ref[:, head * LANES : head * LANES + 1])

    def step(block, causal):
        at = pl.ds(key_row(block, rows, count), rows)
        keys, values = kv_ref[at, :HD], kv_ref[at, HD:]
        bias = key_bias(block, rows, length)
        dk = jnp.zeros((rows, HD), F32)
        dv = jnp.zeros((rows, HD), F32)
        for head in range(H):
            cols = slice(head * HD, (head + 1) * HD)
            query, grad = query_ref[:, cols], grad_ref[:, cols]
            weight = jnp.exp(dot(query, keys, NT) + bias) * inverse[head]
            if causal:
                row = lax.broadcasted_iota(jnp.int32, (rows, rows), 0)
                col = lax.broadcasted_iota(jnp.int32, (rows, rows), 1)
                weight = jnp.where(col <= row, weight, 0.0)
            score = (weight * (dot(grad, values, NT) - delta[head])).astype(BF)
            dq_acc[:, cols] += dot(score, keys)
            dk = dk + dot(score, query, TN)
            dv = dv + dot(weight.astype(BF), grad, TN)
        acc_ref[at, :HD] += dk
        acc_ref[at, HD:] += dv

    def loop(block, carry):
        step(block, False)
        return carry

    lax.fori_loop(0, mine, loop, 0)
    step(mine, True)
    dq_ref[...] = dq_acc[...]

    @pl.when(step_id == pl.num_programs(0) - 1)
    def _():
        dkv_ref[...] = acc_ref[...].astype(BF)


def attend_back(info, query, grad, mixed, total, kv):
    half = query.shape[0] // 2
    spec = lambda cols: pl.BlockSpec((half, cols), lambda i, info: (i, 0))
    full = pl.BlockSpec(kv.shape, lambda i, info: (0, 0))
    return pl.pallas_call(
        attend_back_kernel,
        grid_spec=pltpu.PrefetchScalarGridSpec(
            num_scalar_prefetch=1,
            grid=(2,),
            in_specs=[spec(Q_COLS), spec(Q_COLS), spec(Q_COLS), spec(H * LANES), full],
            out_specs=[spec(Q_COLS), full],
            scratch_shapes=[pltpu.VMEM(kv.shape, F32), pltpu.VMEM((half, Q_COLS), F32)],
        ),
        out_shape=[
            jax.ShapeDtypeStruct((2 * half, Q_COLS), F32),
            jax.ShapeDtypeStruct(kv.shape, BF),
        ],
        compiler_params=pltpu.CompilerParams(vmem_limit_bytes=VMEM_LIMIT),
        cost_estimate=NO_COST,
    )(info, query, grad, mixed, total, kv)


GELU_A = 0.7978845608028654
GELU_B = 0.044715


def mlp_up_kernel(x_ref, own_ref, other_ref, gate_up_ref, hidden_ref):
    units = own_ref.shape[1] // 2
    for k, w_ref in enumerate((own_ref, other_ref)):
        both = dot(x_ref[...], w_ref[...])
        gate_up_ref[:, k * 2 * units : (k + 1) * 2 * units] = both.astype(BF)
        gate, up = both[:, :units], both[:, units:]
        inner = jnp.tanh(GELU_A * gate * (1.0 + GELU_B * gate * gate))
        hidden = (0.5 * gate * (1.0 + inner) * up).astype(BF)
        hidden_ref[:, k * units : (k + 1) * units] = hidden


def mlp_down_kernel(hidden_ref, own_ref, other_ref, part_ref):
    units = own_ref.shape[1]
    total = dot(hidden_ref[:, :units], own_ref[...], NT)
    part_ref[...] = (total + dot(hidden_ref[:, units:], other_ref[...], NT)).astype(BF)


def mlp_tile(rows):
    return min(rows, 512)


def mlp_up(x, own, other):
    rows, width = x.shape
    units = own.shape[1] // 2
    tile = mlp_tile(rows)
    spec = lambda cols: pl.BlockSpec((tile, cols), lambda i: (i, 0))
    return pl.pallas_call(
        mlp_up_kernel,
        grid=(rows // tile,),
        in_specs=[spec(width), whole(own.shape), whole(own.shape)],
        out_specs=[spec(4 * units), spec(2 * units)],
        out_shape=[
            jax.ShapeDtypeStruct((rows, 4 * units), BF),
            jax.ShapeDtypeStruct((rows, 2 * units), BF),
        ],
        compiler_params=pltpu.CompilerParams(vmem_limit_bytes=VMEM_LIMIT),
        cost_estimate=NO_COST,
    )(x, own, other)


def mlp_down(hidden, own, other):
    rows, (width, units) = hidden.shape[0], own.shape
    tile = mlp_tile(rows)
    spec = lambda cols: pl.BlockSpec((tile, cols), lambda i: (i, 0))
    return pl.pallas_call(
        mlp_down_kernel,
        grid=(rows // tile,),
        in_specs=[spec(2 * units), whole(own.shape), whole(own.shape)],
        out_specs=spec(width),
        out_shape=jax.ShapeDtypeStruct((rows, width), BF),
        compiler_params=pltpu.CompilerParams(vmem_limit_bytes=VMEM_LIMIT),
        cost_estimate=NO_COST,
    )(hidden, own, other)


def mlp_back_kernel(
    grad_ref,
    gate_up_ref,
    own_ref,
    other_ref,
    own_down_ref,
    other_down_ref,
    part_ref,
    gate_up_grad_ref,
):
    units = own_down_ref.shape[1]
    total = None
    for k, (w_ref, down_ref) in enumerate(((own_ref, own_down_ref), (other_ref, other_down_ref))):
        base = k * 2 * units
        hidden_grad = dot(grad_ref[...], down_ref[...])
        gate = gate_up_ref[:, base : base + units].astype(F32)
        up = gate_up_ref[:, base + units : base + 2 * units].astype(F32)
        square = gate * gate
        inner = jnp.tanh(GELU_A * gate * (1.0 + GELU_B * square))
        half = 0.5 * (1.0 + inner)
        slope = half + 0.5 * gate * (1.0 - inner * inner) * (
            GELU_A * (1.0 + 3.0 * GELU_B * square)
        )
        gate_grad = (hidden_grad * up * slope).astype(BF)
        up_grad = (hidden_grad * (gate * half)).astype(BF)
        gate_up_grad_ref[:, base : base + units] = gate_grad
        gate_up_grad_ref[:, base + units : base + 2 * units] = up_grad
        part = dot(gate_up_grad_ref[:, base : base + 2 * units], w_ref[...], NT)
        total = part if total is None else total + part
    part_ref[...] = total.astype(BF)


def mlp_backward(grad, gate_up, weights):
    rows, width = grad.shape
    units = weights[2].shape[1]
    tile = mlp_tile(rows)
    spec = lambda cols: pl.BlockSpec((tile, cols), lambda i: (i, 0))
    return pl.pallas_call(
        mlp_back_kernel,
        grid=(rows // tile,),
        in_specs=[spec(width), spec(4 * units)] + [whole(w.shape) for w in weights],
        out_specs=[spec(width), spec(4 * units)],
        out_shape=[
            jax.ShapeDtypeStruct((rows, width), BF),
            jax.ShapeDtypeStruct((rows, 4 * units), BF),
        ],
        compiler_params=pltpu.CompilerParams(vmem_limit_bytes=VMEM_LIMIT),
        cost_estimate=NO_COST,
    )(grad, gate_up, *weights)


def products(lefts, rights, units, kind):
    rows, width = lefts[0].shape
    kinds = rights[0].shape[1] // (2 * units)
    left = pl.BlockSpec((rows, width), lambda j: (0, 0))
    right = pl.BlockSpec((rows, units), lambda j: (0, kind + kinds * (1 - j)))
    out = pl.BlockSpec((width, units), lambda j: (0, 0))
    shape = jax.ShapeDtypeStruct((width, units), BF)

    def kernel(*refs):
        left_refs, right_refs, (other_ref, own_ref, turned_ref) = refs[:2], refs[2:4], refs[4:]

        @pl.when(pl.program_id(0) == 0)
        def _():
            for k in range(2):
                turned_ref[:, k * rows : (k + 1) * rows] = left_refs[k][...].T

        total = dot(turned_ref[:, :rows], right_refs[0][...])
        total = (total + dot(turned_ref[:, rows:], right_refs[1][...])).astype(BF)

        @pl.when(pl.program_id(0) == 0)
        def _():
            other_ref[...] = total

        @pl.when(pl.program_id(0) == 1)
        def _():
            own_ref[...] = total

    return pl.pallas_call(
        kernel,
        grid=(2,),
        in_specs=[left, left, right, right],
        out_specs=[out, out],
        out_shape=[shape, shape],
        scratch_shapes=[pltpu.VMEM((width, 2 * rows), BF)],
        compiler_params=pltpu.CompilerParams(vmem_limit_bytes=VMEM_LIMIT),
        cost_estimate=NO_COST,
    )(*lefts, *rights)


def body(
    layer_input,
    cotangent,
    lengths,
    weights,
    norm_gains,
    head_gains,
    moment_weights,
    moment_gains,
    moment_head,
    square_weights,
    square_gains,
    square_head,
):
    rows = weights.shape[0]
    head_rows = head_gains.shape[0]
    width = layer_input.shape[1]
    dp_count, z_count = lax.axis_size("dp"), lax.axis_size("ctx")
    units = -(-FF // (dp_count * LANES)) * LANES

    weights_low = weights.astype(BF)
    gain_cols = jnp.zeros((max(rows, head_rows), LANES), BF)
    gain_cols = gain_cols.at[:rows, :4].set(norm_gains.astype(BF))
    gain_cols = gain_cols.at[:head_rows, 4:6].set(head_gains.astype(BF))[:rows]
    first_shard = jnp.concatenate([weights_low[:, :START_GATE], pad_cols(gain_cols, 2 * LANES)], axis=1)
    mlp_shard = jnp.concatenate(
        [
            pad_cols(weights_low[:, start : start + FF], dp_count * units)
            .reshape(rows, dp_count, units)
            .transpose(1, 0, 2)
            for start in (START_GATE, START_GATE + FF, START_DOWN)
        ],
        axis=2,
    )
    mlp_block = lax.all_to_all(mlp_shard, "dp", split_axis=0, concat_axis=0, tiled=True)
    mlp_block = mlp_block.reshape(dp_count * rows, 3 * units)
    gate_up_block = mlp_block[:, : 2 * units]
    gate_up_own = lax.all_gather(gate_up_block, "ctx", axis=0, tiled=True)
    first_full = gather_rows(first_shard, gate_up_block)
    w_qkv = first_full[:, :START_GATE]
    gain_part = first_full[:, START_GATE : START_GATE + LANES].astype(F32)
    gain_f = 1.0 + gain_part[:, :4]
    head_f = gain_part.reshape(z_count, dp_count, rows, LANES)[:, :, :head_rows, 4:6]
    head_f = 1.0 + head_f.transpose(1, 0, 2, 3).reshape(HD, 2)

    order = np.arange(width).reshape(dp_count, z_count, rows).transpose(1, 0, 2).reshape(width)
    place = (jnp.arange(width)[:, None] == jnp.asarray(order)[None, :]).astype(BF)

    tok_rows = layer_input.shape[0]
    ctx_count = z_count
    local_slots = lax.axis_index("ctx") * tok_rows + jnp.arange(tok_rows, dtype=jnp.int32)
    positions = block_positions(local_slots, tok_rows, ctx_count)
    seq_length = lengths[0]
    row_valid = positions < seq_length
    inputs = jnp.dot(layer_input, place, preferred_element_type=F32)
    cot = jnp.dot(cotangent, place, preferred_element_type=F32)
    normed_in, pull_in = jax.vjp(rms_gain, inputs, gain_f[:, 0])
    normed_low = normed_in.astype(BF)
    key_value_raw = jnp.dot(normed_low, w_qkv[:, Q_COLS:], preferred_element_type=F32)
    query_raw = jnp.dot(normed_low, w_qkv[:, :Q_COLS], preferred_element_type=F32)

    def query_part(query_arg, head_arg):
        return (
            rotate(rms_gain(query_arg.reshape(tok_rows, H, HD), head_arg), positions) * QUERY_SCALE
        )

    def key_part(key_arg, head_arg):
        return rotate(rms_gain(key_arg[:, None, :], head_arg), positions)[:, 0]

    keys, pull_key = jax.vjp(key_part, key_value_raw[:, :HD], head_f[:, 1])
    key_value = jnp.concatenate([keys.astype(BF), key_value_raw[:, HD:].astype(BF)], axis=1)
    w_out = gather_rows(tie(weights_low[:, START_OUT:START_DOWN], first_full))
    queries, pull_query = jax.vjp(query_part, query_raw, head_f[:, 0])
    query_low = queries.astype(BF).reshape(tok_rows, Q_COLS)
    key_value = tie_all(key_value, [gate_up_own, w_out, query_low])
    key_value = lax.all_gather(key_value, "ctx", axis=0, tiled=True)
    down_own = lax.all_gather(
        tie(mlp_block[:, 2 * units :], key_value), "ctx", axis=0, tiled=True
    )
    gate_up_weights = (gate_up_own, flip(gate_up_own, 1))
    info = jnp.stack([lax.axis_index("ctx"), seq_length]).astype(jnp.int32)
    mixed_low, inverse_total = attend(info, query_low, key_value)
    attn_proj = jnp.einsum("tc,dc->td", mixed_low, w_out, preferred_element_type=F32)
    post_attn, pull_attn = jax.vjp(rms_gain, attn_proj, gain_f[:, 1])
    residual_mid = inputs + post_attn
    normed_mid, pull_mid = jax.vjp(rms_gain, residual_mid, gain_f[:, 2])

    mid_low = normed_mid.astype(BF)
    out_grad = cot * row_valid[:, None].astype(F32)
    chunks = 2
    size = tok_rows // chunks
    spans = [slice(i * size, (i + 1) * size) for i in range(chunks)]
    assert chunks == 2
    mids = [None, None]
    starts = [spread_start(mid_low[span]) for span in spans]
    mids[0] = jnp.concatenate(spread_end(starts[0]), axis=0)
    mids[0] = tie_all(mids[0], starts[1] + [down_own])
    second = spread_end(starts[1])
    first_up = mlp_up(mids[0], *gate_up_weights)
    mids[1] = tie(jnp.concatenate(second, axis=0), first_up[1])
    forward = [first_up, mlp_up(mids[1], *gate_up_weights)]
    gate_ups, hiddens = (list(kind) for kind in zip(*forward))
    down_own = tie(down_own, mids[1])
    mlp_weights = gate_up_weights + (down_own, flip(down_own, 1))
    hiddens[0] = tie(hiddens[0], gate_ups[1])
    parts = [mlp_down(hiddens[0], *mlp_weights[2:])]
    first, sent = collect(parts[0])
    hiddens[1] = tie_all(hiddens[1], sent[0])
    parts.append(mlp_down(hiddens[1], *mlp_weights[2:]))
    grad_three = 0.0
    output_low, starts = [], []
    for i, span in enumerate(spans):
        mlp_proj = collect(parts[1], starts[0][0])[0] if i else first
        post_mlp, pull_mlp = jax.vjp(rms_gain, mlp_proj, gain_f[:, 3])
        output_low.append((residual_mid[span] + post_mlp).astype(BF))
        mlp_grad, gain_part_three = pull_mlp(out_grad[span])
        grad_three = grad_three + gain_part_three
        starts.append(spread_start(mlp_grad.astype(BF)))
    output_low = jnp.concatenate(output_low, axis=0)
    mlp_grads = [jnp.concatenate(spread_end(starts[0]), axis=0)]
    starts[1] = [tie(part, mlp_grads[0]) for part in starts[1]]
    mlp_grads[0] = tie(tie(mlp_grads[0], starts[1][0]), starts[1][1])
    second = spread_end(starts[1])

    def both_cores(other, own):
        return (own.astype(F32) + flip(other, 1).astype(F32)).astype(BF)

    def shard_sum(grad):
        return lax.psum_scatter(grad, "ctx", scatter_dimension=0, tiled=True)

    def to_rows(summed):
        return lax.all_to_all(
            summed.reshape(dp_count, rows, summed.shape[1]), "dp", 0, 0, tiled=True
        )

    backward = [mlp_backward(mlp_grads[0], gate_ups[0], mlp_weights)]
    mlp_grads.append(jnp.concatenate(second, axis=0))
    first, sent = collect(backward[0][0])
    hiddens = [tie_all(hidden, sent[0]) for hidden in hiddens]
    down_other, down_mine = products(mlp_grads, hiddens, units, 0)
    down_grad = both_cores(down_other, tie_all(down_mine, sent[1]))
    summed_down = shard_sum(down_grad)
    backward.append(mlp_backward(mlp_grads[1], tie(gate_ups[1], down_mine), mlp_weights))
    second, sent = collect(backward[1][0])
    mid_grad = jnp.concatenate([first, second], axis=0)
    gate_up_grads = [tie_all(grad, sent[1]) for _, grad in backward]
    gate_other, gate_mine = products(mids, gate_up_grads, units, 0)
    gate_grad = both_cores(gate_other, gate_mine)
    summed_gate = shard_sum(gate_grad)
    output = lax.dot_general(
        tie(output_low, gate_mine), place, NT, preferred_element_type=F32
    ).astype(BF)

    mid_grad = tie_all(mid_grad, [gate_mine, summed_down, output])
    resid_part, grad_two = pull_mid(mid_grad)
    residual_grad = out_grad + resid_part
    attn_grad, grad_one = pull_attn(residual_grad)
    attn_low = attn_grad.astype(BF)
    mixed_grad = jnp.dot(attn_low, w_out, preferred_element_type=F32).astype(BF)
    query_grads, key_value_part = attend_back(
        info, query_low, mixed_grad, mixed_low, inverse_total, key_value
    )
    key_value_grad = lax.psum_scatter(
        tie(key_value_part, summed_gate), "ctx", scatter_dimension=0, tiled=True
    ).astype(F32)
    gate_up_grads = [tie(grad, query_grads) for grad in gate_up_grads]
    up_other, up_mine = products(mids, gate_up_grads, units, 1)
    up_grad = both_cores(up_other, up_mine)
    attn_late = tie(attn_low, query_grads)
    summed_up = shard_sum(tie(up_grad, key_value_grad))

    raw_query, grad_head_query = pull_query(query_grads.reshape(tok_rows, H, HD))
    query_grad_low = raw_query.astype(BF)
    bits_out, bits_query = ([1] + bits[::-1] for bits in chip_orders())
    out_share = scatter_cols(dot(attn_late, mixed_low, TN), bits_out)
    query_share = scatter_cols(dot(normed_low, query_grad_low, TN), bits_query)

    key_value_grad = tie(key_value_grad, up_grad)
    raw_key, grad_head_key = pull_key(key_value_grad[:, :HD])
    key_value_low = jnp.concatenate([raw_key, key_value_grad[:, HD:]], axis=1).astype(BF)
    late_bits, same_bits = bits_out[:2], bits_out[2:]
    late_share, sent = scatter_cols_sent(dot(normed_low, key_value_low, TN), late_bits[:1])
    in_part = dot(query_grad_low, w_qkv[:, :Q_COLS], NT)
    in_part = in_part + dot(tie(key_value_low, sent), w_qkv[:, Q_COLS:], NT)
    input_part, grad_zero = pull_in(in_part)
    grad_input_low = (residual_grad + input_part).astype(BF)

    back = to_rows(jnp.concatenate([summed_gate, summed_up, summed_down], axis=1))
    early = shard_sum(jnp.concatenate([query_share, out_share], axis=1))
    slices = scatter_parts(late_share.reshape(z_count, -1, late_share.shape[1]), "ctx")
    late_rows = tie(scatter_direct(slices, "ctx").astype(BF), early)
    late_rows = scatter_cols(late_rows, late_bits[1:])
    for bit in same_bits:
        late_rows = (late_rows.astype(F32) + flip(late_rows, bit).astype(F32)).astype(BF)
    back_attn = jnp.concatenate([early, late_rows], axis=1)
    back_attn = to_rows(back_attn)
    share = Q_COLS // dp_count
    sum_query = columns_back(back_attn[:, :, :share], bits_query)
    sum_out = columns_back(back_attn[:, :, share : 2 * share], bits_out)
    back_late = back_attn[:, :, 2 * share :]
    back_late = back_late.reshape((2,) * len(bits_out) + back_late.shape[1:])
    for bit in sorted(same_bits):
        back_late = back_late[(slice(None),) * (len(bits_out) - bit.bit_length()) + (0,)]
    back_late = back_late.reshape((-1,) + back_late.shape[-2:])
    sum_late = columns_back(back_late, late_bits)

    gains = jnp.stack([grad_zero, grad_one, grad_two, grad_three]).reshape(-1)
    gains = jnp.concatenate([gains, grad_head_query, grad_head_key]).reshape(-1, LANES)
    for bit in bits_out:
        gains = gains + flip(gains, bit)
    gains = sum(shift(gains, "ctx", distance) for distance in range(1, z_count)) + gains
    gains = gains.reshape(-1)
    dp_me, z_me = lax.axis_index("dp"), lax.axis_index("ctx")
    sum_gains = lax.dynamic_slice_in_dim(
        gains[: 4 * width].reshape(4, width), (z_me * dp_count + dp_me) * rows, rows, 1
    ).T
    sum_head = lax.dynamic_slice_in_dim(
        gains[4 * width :].reshape(2, HD), (dp_me * z_count + z_me) * head_rows, head_rows, 1
    ).T
    sum_gate, sum_up, sum_down = (
        back[:, :, at : at + units]
        .transpose(1, 0, 2)
        .reshape(rows, dp_count * units)[:, :FF]
        .astype(F32)
        for at in (0, units, 2 * units)
    )

    grad_input = lax.dot_general(
        grad_input_low, place, (((1,), (1,)), ((), ())), preferred_element_type=F32
    ).astype(BF)

    sum_weights = jnp.concatenate(
        [sum_query, sum_late, sum_gate, sum_up, sum_out, sum_down], axis=1
    )
    new_w, first_w, second_w = adamw(
        weights, sum_weights, moment_weights, square_weights, RATE_WEIGHTS, WEIGHT_DECAY
    )
    new_g, first_g, second_g = adamw(
        norm_gains, sum_gains, moment_gains, square_gains, RATE_GAINS, 0.0
    )
    new_h, first_h, second_h = adamw(
        head_gains, sum_head, moment_head, square_head, RATE_GAINS, 0.0
    )
    return (
        output,
        grad_input,
        new_w,
        new_g,
        new_h,
        first_w,
        first_g,
        first_h,
        second_w,
        second_g,
        second_h,
        new_w.astype(BF),
    )


def solution(mesh):
    rows = P(("dp", "ctx"), None)
    in_specs = (rows, rows, P("dp")) + (rows,) * 9
    return jax.shard_map(
        body, mesh=mesh, in_specs=in_specs, out_specs=(rows,) * 12, check_vma=False
    )
```
